128 devices in a mesh: dir: 32 (over x, z, core), slab: 4 (over y).
Axes of the slice: x: 4, y: 4, z: 4, core: 2. Of those that a mesh axis runs over, the one named last changes fastest.
Arguments:
- child_field: float32 [4, 1024, 2, 2048], P('slab', 'dir'), may hold values from -6 to 6
- child_src: int32 [4, 1024, 24], P('slab', 'dir'), may hold values from 0 to 1023
- child_type: int32 [4, 1024, 24], P('slab', 'dir'), may hold values from 0 to 159
- child_table: float32 [160, 2, 2048], replicated, may hold values from -2 to 2
- child_parent: int32 [4, 1024], P('slab', 'dir'), may hold values from 0 to 127
- child_octant: int32 [4, 1024], P('slab', 'dir'), may hold values from 0 to 7
- theta_interp: float32 [64, 32], replicated, may hold values from -1 to 1
- phi_interp: float32 [128, 64], replicated, may hold values from -0.75 to 0.75
- shift_table: float32 [8, 2, 8192], replicated, may hold values from -4 to 4
- readers: int32 [4, 2, 32], P('slab'), may hold values from 0 to 127
- parent_src: int32 [4, 128, 24], P('slab'), may hold values from 0 to 191
- parent_type: int32 [4, 128, 24], P('slab'), may hold values from 0 to 159
- parent_table: float32 [160, 2, 8192], P(None, None, 'dir'), may hold values from -2 to 2
Outputs:
- child_local: float32 [4, 1024, 2, 2048], P('slab', 'dir')
- parent_local: float32 [4, 128, 2, 8192], P('slab', None, None, 'dir')
The draws below stay inside these ranges and needn't reach their ends.
Inputs may be any that keep to these rules, and one draw needn't show every extreme that they name: `child_src`: indices of child boxes of the same slab. `child_parent`: indices of parents of the same slab. `readers`: indices of parents of the sending slab.
All inputs are finite; a program needn't handle non-finite values.
Results may differ from the reference program's by a relative error of at most 0.00007.
Values sent between devices are 32-bit elements; how exact they have to be, the bound alone decides.
No kernel may reach another device: no remote copies, remote signals or barrier semaphores. Data moves between devices by JAX's collectives and lax.ppermute only.
A program may use at most 192 MiB of HBM per device.

```python
import math
import jax
import jax.numpy as jnp
import numpy as np
from jax import lax

KTC = 32
KFC = 64
KTP = 64
KFP = 128
KC = 2048
KP = 8192
NTC = 160
NTP = 160
LC = 24
LP = 24
SLABS = 4
SLAB_CH = 1024
PS = 128
BR = 32


def plant(array, own_key, least, top_value):
    longest = array.shape.index(max(array.shape))
    spots = []
    for shift in (0, 1):
        where = [jax.random.randint(jax.random.fold_in(own_key, axis), (), 0, length) for axis, length in enumerate(array.shape)]
        where[longest] = (where[longest] + shift) % array.shape[longest]
        spots.append(tuple(where))
    return array.at[spots[0]].set(least).at[spots[1]].set(top_value)


def levels(stream_key, extent, shards, least, top_value):
    factor_of = 1.0
    for axis_at, blocks in shards:
        heights = jax.random.uniform(jax.random.fold_in(jax.random.fold_in(stream_key, 6), axis_at), (blocks,), jnp.float32, least / len(shards), top_value / len(shards))
        factor_of = factor_of * jnp.repeat(jnp.exp(heights), extent[axis_at] // blocks).reshape((-1,) + (1,) * (len(extent) - 1 - axis_at))
    return factor_of


def rank_bounds(number_of, slope):
    portions = [(1 << 20) // math.isqrt(rank ** slope) + 1 for rank in range(1, number_of + 1)]
    spread = 1 + sum(portions) // (1 << 30)
    return np.cumsum(np.array([max(1, weight // spread) for weight in portions]))


def ranked(stream_key, shape, number_of, lean):
    table = rank_bounds(number_of, lean)
    lot = jax.random.randint(jax.random.fold_in(stream_key, 1), shape, 0, int(table[number_of - 1]))
    grade = jnp.searchsorted(jnp.asarray(table, jnp.int32), lot, side="right")
    return jax.random.permutation(jax.random.fold_in(stream_key, 2), number_of)[grade].astype(jnp.int32)


def scatter_about(own_key, dims, spread, bound, shards=(), kind=jnp.bfloat16):
    array = jax.random.normal(own_key, dims, jnp.float32) * spread
    if len(shards) > 0:
        array = levels(own_key, dims, shards, -0.22, 0.18) * array
    return jnp.clip(array, min=-bound, max=bound).astype(kind)


def setup_inputs(seed: int = 0) -> dict:
    seeds = jax.random.split(jax.random.key(seed), 14)
    return {
        "child_field": scatter_about(seeds[0], (SLABS, SLAB_CH, 2, KC), 1.0, 6.0, ((0, 4), (1, 32)), jnp.float32),
        "child_src": plant(ranked(seeds[1], (SLABS, SLAB_CH, LC), SLAB_CH, 2), jax.random.fold_in(seeds[1], 3), 0, SLAB_CH - 1).astype(jnp.int32),
        "child_type": plant(jax.random.randint(seeds[2], (SLABS, SLAB_CH, LC), 0, NTC), jax.random.fold_in(seeds[2], 1), 0, NTC - 1).astype(jnp.int32),
        "child_table": scatter_about(seeds[3], (NTC, 2, KC), 0.15, 2.0, (), jnp.float32),
        "child_parent": plant(jax.random.randint(seeds[4], (SLABS, SLAB_CH), 0, PS), jax.random.fold_in(seeds[4], 1), 0, PS - 1).astype(jnp.int32),
        "child_octant": plant(jax.random.randint(seeds[5], (SLABS, SLAB_CH), 0, 8), jax.random.fold_in(seeds[5], 1), 0, 7).astype(jnp.int32),
        "theta_interp": scatter_about(seeds[6], (KTP, KTC), KTC ** -0.5, 1.0, (), jnp.float32),
        "phi_interp": scatter_about(seeds[7], (KFP, KFC), KFC ** -0.5, 0.75, (), jnp.float32),
        "shift_table": scatter_about(seeds[8], (8, 2, KP), 0.25, 4.0, (), jnp.float32),
        "readers": plant(jax.random.randint(seeds[9], (SLABS, 2, BR), 0, PS), jax.random.fold_in(seeds[9], 1), 0, PS - 1).astype(jnp.int32),
        "parent_src": plant(jax.random.randint(seeds[10], (SLABS, PS, LP), 0, PS + 2 * BR), jax.random.fold_in(seeds[10], 1), 0, (PS + 2 * BR) - 1).astype(jnp.int32),
        "parent_type": plant(jax.random.randint(seeds[11], (SLABS, PS, LP), 0, NTP), jax.random.fold_in(seeds[11], 1), 0, NTP - 1).astype(jnp.int32),
        "parent_table": scatter_about(seeds[12], (NTP, 2, KP), 0.15, 2.0, ((2, 32),), jnp.float32),
    }


def translate(fields, tables, sources, entry_types):
    picked = fields[sources]
    weights = tables[entry_types]
    real_part = jnp.sum(weights[..., 0, :] * picked[..., 0, :] - weights[..., 1, :] * picked[..., 1, :], axis=-2)
    imag_part = jnp.sum(weights[..., 0, :] * picked[..., 1, :] + weights[..., 1, :] * picked[..., 0, :], axis=-2)
    return jnp.stack([real_part, imag_part], axis=-2)


def interpolate(field, theta_interp, phi_interp):
    leading = field.shape[:-1]
    grid_child = field.reshape(leading + (theta_interp.shape[1], phi_interp.shape[1]))
    finer = jnp.einsum('pt,...tf->...pf', theta_interp, grid_child, precision=lax.Precision.HIGHEST)
    finest = jnp.einsum('qf,...pf->...pq', phi_interp, finer, precision=lax.Precision.HIGHEST)
    return finest.reshape(leading + (-1,))


def apply_shift(values, shifts):
    real_part = shifts[..., 0, :] * values[..., 0, :] - shifts[..., 1, :] * values[..., 1, :]
    imag_part = shifts[..., 0, :] * values[..., 1, :] + shifts[..., 1, :] * values[..., 0, :]
    return jnp.stack([real_part, imag_part], axis=-2)


def reference(child_field, child_src, child_type, child_table, child_parent, child_octant, theta_interp, phi_interp, shift_table, readers, parent_src, parent_type, parent_table):
    flat_field = child_field.reshape(SLABS * SLAB_CH, 2, KC)
    offsets = (jnp.arange(SLABS, dtype=jnp.int32) * SLAB_CH)[:, None, None]
    global_src = (child_src + offsets).reshape(SLABS * SLAB_CH, LC)
    flat_types = child_type.reshape(SLABS * SLAB_CH, LC)

    def child_entry(inputs):
        return translate(flat_field, child_table, inputs[0], inputs[1])

    child_local = lax.map(child_entry, (global_src, flat_types)).reshape(SLABS, SLAB_CH, 2, KC)

    shifted = apply_shift(interpolate(child_field, theta_interp, phi_interp), shift_table[child_octant])
    onehot = (child_parent[:, :, None] == jnp.arange(PS, dtype=jnp.int32)[None, None, :]).astype(jnp.float32)
    parent_field = jnp.einsum('scp,scxk->spxk', onehot, shifted, precision=lax.Precision.HIGHEST)

    up_blocks = jax.vmap(lambda fld, idx: fld[idx])(parent_field, readers[:, 0])
    down_blocks = jax.vmap(lambda fld, idx: fld[idx])(parent_field, readers[:, 1])
    zero_block = jnp.zeros((1, BR, 2, KP), jnp.float32)
    from_lower = jnp.concatenate([zero_block, up_blocks[:-1]], axis=0)
    from_upper = jnp.concatenate([down_blocks[1:], zero_block], axis=0)
    extended = jnp.concatenate([parent_field, from_lower, from_upper], axis=1)
    flat_ext = extended.reshape(SLABS * (PS + 2 * BR), 2, KP)
    parent_offsets = (jnp.arange(SLABS, dtype=jnp.int32) * (PS + 2 * BR))[:, None, None]
    parent_global = (parent_src + parent_offsets).reshape(SLABS * PS, LP)
    parent_types = parent_type.reshape(SLABS * PS, LP)

    def parent_entry(inputs):
        return translate(flat_ext, parent_table, inputs[0], inputs[1])

    parent_local = lax.map(parent_entry, (parent_global, parent_types)).reshape(SLABS, PS, 2, KP)
    return (child_local, parent_local)
```

```python
import functools

import jax
import jax.numpy as jnp
from jax import lax
from jax.experimental import pallas as pl
from jax.experimental.pallas import tpu as pltpu
from jax.sharding import PartitionSpec as P

F32 = jnp.float32
BF16 = jnp.bfloat16
LANES = 128
HALF = 64
DIRS = 32
BOXES = 32
SLAB = DIRS * BOXES
ENTRIES = 24
TYPES = 160
PARENTS = 128
BORDER = 32
OCTANTS = 8
LIST_ROWS = ENTRIES * BOXES // LANES
AT_TYPE = BOXES + LIST_ROWS
AT_OWNER = AT_TYPE + LIST_ROWS
SENT = 48


def params(flops, nbytes):
    return dict(
        compiler_params=pltpu.CompilerParams(vmem_limit_bytes=40 << 20),
        cost_estimate=pl.CostEstimate(flops=flops, bytes_accessed=nbytes, transcendentals=0),
    )


def lane_ids(rows):
    return lax.broadcasted_iota(jnp.int32, (rows, LANES), 1)


def swap_halves(value):
    return pltpu.roll(value, HALF, 1)


def split(value):
    high = value.astype(BF16)
    return high, (value - high.astype(F32)).astype(BF16)


def turned(value):
    rows, columns = value.shape
    wide = jnp.concatenate([value, jnp.zeros((rows, LANES - columns), F32)], axis=1)
    return jnp.transpose(jnp.concatenate([wide, jnp.zeros((LANES - rows, LANES), F32)], axis=0))


def pack_kernel(field, src, kind, parent, octant, out, work):
    low = lane_ids(BOXES) < HALF
    for pair in range(DIRS // 2):
        real = field[:, 0, pair * LANES : (pair + 1) * LANES]
        imag = field[:, 1, pair * LANES : (pair + 1) * LANES]
        out[2 * pair, 0:BOXES, :] = jnp.where(low, real, swap_halves(imag))
        out[2 * pair + 1, 0:BOXES, :] = jnp.where(low, swap_halves(real), imag)
    chunk = lane_ids(LIST_ROWS) // BOXES
    for at, ref in ((0, src), (ENTRIES, kind)):
        work[0:LANES, :] = turned(ref[...].astype(F32))
        rows = jnp.zeros((LIST_ROWS, LANES), F32)
        for part in range(4):
            picked = work[pl.ds(part, LIST_ROWS, stride=4), :]
            rows = jnp.where(chunk == part, pltpu.roll(picked, part * BOXES, 1), rows)
        work[LANES + at : LANES + at + LIST_ROWS, :] = rows
    first = work[LANES : LANES + LIST_ROWS, :]
    second = work[LANES + ENTRIES : LANES + ENTRIES + LIST_ROWS, :]
    owners = []
    for ref in (parent, octant):
        value = ref[...].astype(F32)
        owners.append(jnp.concatenate([value] * 4, axis=1))
    tail = jnp.concatenate(
        [first, second] + owners + [jnp.zeros((SENT - AT_OWNER - 2, LANES), F32)], axis=0
    )
    for device in range(DIRS):
        out[device, BOXES:SENT, :] = tail


def polar_kernel(packed, theta, out):
    columns = [packed[pl.ds(c, DIRS, stride=SENT), :] for c in range(BOXES)]
    fields = jnp.concatenate(columns, axis=1)
    high, low = split(fields)
    theta_high, theta_low = split(theta[...])
    left = jnp.concatenate([theta_high, theta_high, theta_low], axis=1)
    right = jnp.concatenate([high, low, high], axis=0)
    finer = jnp.dot(left, right, preferred_element_type=F32)
    for c in range(BOXES):
        out[pl.ds(c, 2 * DIRS, stride=BOXES), :] = finer[:, c * LANES : (c + 1) * LANES]


def tables_kernel(me, child, parent, child_out, parent_out):
    odd = lax.rem(me[0], 2) == 1
    low = lane_ids(TYPES) < HALF
    real, imag = child[:, 0, :], child[:, 1, :]
    even_rows = jnp.where(low, real, swap_halves(imag))
    odd_rows = jnp.where(low, swap_halves(real), imag)
    rows = jnp.where(odd, odd_rows, even_rows)
    rows = jnp.concatenate([rows, jnp.zeros((2 * LANES - TYPES, LANES), F32)], axis=0)
    child_out[...] = jnp.transpose(rows)
    for polar in range(2):
        real = parent[:, 0, polar * LANES : (polar + 1) * LANES]
        imag = parent[:, 1, polar * LANES : (polar + 1) * LANES]
        for at, value in ((0, real), (1, real), (4, -imag), (5, imag)):
            parent_out[pl.ds(at + 2 * polar, TYPES, stride=8), :] = value


def child_kernel(got, table, out, src, kind):
    chunk = lane_ids(8) // BOXES
    for at, ref in ((BOXES, src), (AT_TYPE, kind)):
        for row in range(LIST_ROWS):
            rows = [got[pl.ds(i * SENT + at + row, 8, stride=4 * SENT), :] for i in range(4)]
            for part in range(4):
                total = jnp.zeros((8, LANES), F32)
                for i in range(4):
                    moved = rows[i] if i == part else pltpu.roll(rows[i], ((i - part) % 4) * BOXES, 1)
                    total = jnp.where(chunk == i, moved, total)
                ref[4 * row + part] = total.astype(jnp.int32)
    fields = jnp.concatenate([got[d * SENT : d * SENT + BOXES, :] for d in range(DIRS)], axis=0)
    fields = jnp.concatenate(split(jnp.transpose(fields)), axis=0)
    weights = jnp.concatenate(split(table[...]), axis=0)

    def step(entry, totals):
        real, imag = totals
        wanted, kinds = src[entry], kind[entry]
        wanted = jnp.concatenate([wanted[k : k + 1] for k in range(8)], axis=1)
        kinds = jnp.concatenate([kinds[k : k + 1] for k in range(8)], axis=1)
        hot = (lax.broadcasted_iota(jnp.int32, (SLAB, SLAB), 0) == wanted).astype(F32).astype(BF16)
        hot_kind = (lax.broadcasted_iota(jnp.int32, (2 * LANES, SLAB), 0) == kinds).astype(F32).astype(BF16)
        picked = jnp.dot(fields, hot, preferred_element_type=F32)
        weight = jnp.dot(weights, hot_kind, preferred_element_type=F32)
        picked = picked[:LANES] + picked[LANES:]
        weight = weight[:LANES] + weight[LANES:]
        fr, fi, wr, wi = picked[:HALF], picked[HALF:], weight[:HALF], weight[HALF:]
        return real + (wr * fr - wi * fi), imag + (wr * fi + wi * fr)

    zero = jnp.zeros((HALF, SLAB), F32)
    real, imag = lax.fori_loop(0, ENTRIES, step, (zero, zero))
    out[...] = jnp.transpose(jnp.concatenate([real, imag], axis=0))


def unpack_kernel(got, out):
    low = lane_ids(BOXES) < HALF
    for pair in range(DIRS // 2):
        first, second = got[2 * pair], got[2 * pair + 1]
        out[:, 0, pair * LANES : (pair + 1) * LANES] = jnp.where(low, first, swap_halves(second))
        out[:, 1, pair * LANES : (pair + 1) * LANES] = jnp.where(low, swap_halves(first), second)


def field_kernel(me, got, owner, phi, shifts, readers, out, up, down, work):
    chunk = lane_ids(8) // BOXES
    code = jnp.zeros((8, LANES), F32)
    for i in range(4):
        at = i * SENT + AT_OWNER
        parent = owner[pl.ds(at, 8, stride=4 * SENT), :]
        octant = owner[pl.ds(at + 1, 8, stride=4 * SENT), :]
        code = jnp.where(chunk == i, octant * PARENTS + parent, code)
    code = code.astype(jnp.int32)
    code = jnp.concatenate([code[k : k + 1] for k in range(8)], axis=1)
    hot = (lax.broadcasted_iota(jnp.int32, (OCTANTS * PARENTS, SLAB), 0) == code).astype(F32).astype(BF16)
    halves = []
    for polar in range(2):
        rows = [got[d, polar * BOXES : (polar + 1) * BOXES, :] for d in range(DIRS)]
        halves.extend(split(jnp.concatenate(rows, axis=0)))
    sums = jnp.dot(hot, jnp.concatenate(halves, axis=1), preferred_element_type=F32)
    turn = jnp.transpose(jnp.concatenate([phi[...], jnp.zeros((LANES, HALF), F32)], axis=1))[:HALF]
    none = jnp.zeros((HALF, LANES), F32)
    both = jnp.concatenate(
        [jnp.concatenate([turn, none], axis=1), jnp.concatenate([none, turn], axis=1)], axis=0
    )
    both_high, both_low = split(both)
    right = jnp.concatenate([both_high, both_high, both_low], axis=0)
    for polar in range(2):
        base = 2 * LANES * polar
        high, low = split(sums[:, base : base + LANES] + sums[:, base + LANES : base + 2 * LANES])
        fine = jnp.dot(jnp.concatenate([high, low, high], axis=1), right, preferred_element_type=F32)
        real = jnp.zeros((PARENTS, LANES), F32)
        imag = jnp.zeros((PARENTS, LANES), F32)
        for o in range(OCTANTS):
            fr = fine[o * PARENTS : (o + 1) * PARENTS, :LANES]
            fi = fine[o * PARENTS : (o + 1) * PARENTS, LANES:]
            sr = shifts[o, 0:1, polar * LANES : (polar + 1) * LANES]
            si = shifts[o, 1:2, polar * LANES : (polar + 1) * LANES]
            real += sr * fr - si * fi
            imag += sr * fi + si * fr
        for at, value in ((0, real), (1, imag), (4, imag), (5, real)):
            work[pl.ds(at + 2 * polar, PARENTS, stride=8), :] = value
    out[...] = work[...]

    def copy(i, carry):
        for row, ref in ((0, up), (1, down)):
            at = pl.multiple_of(readers[row, i] * 8, 8)
            ref[pl.ds(pl.multiple_of(i * 8, 8), 8), :] = work[pl.ds(at, 8), :]
        return carry

    lax.fori_loop(0, BORDER, copy, 0)


def parent_kernel(src, kind, own, lower, upper, table, out, rows):
    rows[0 : PARENTS * 8, :] = own[...]
    rows[PARENTS * 8 : (PARENTS + BORDER) * 8, :] = lower[...]
    rows[(PARENTS + BORDER) * 8 :, :] = upper[...]

    def step(p, carry):
        totals = [jnp.zeros((8, LANES), F32) for _ in range(4)]
        for j in range(ENTRIES):
            field = rows[pl.ds(pl.multiple_of(src[p, j] * 8, 8), 8), :]
            weight = table[pl.ds(pl.multiple_of(kind[p, j] * 8, 8), 8), :]
            totals[j % 4] += weight * field
        total = (totals[0] + totals[1]) + (totals[2] + totals[3])
        total = total[:4] + total[4:]
        out[p, :, 0:LANES] = total[0:2]
        out[p, :, LANES:] = total[2:4]
        return carry

    lax.fori_loop(0, PARENTS, step, 0)


def shaped(*shape):
    return jax.ShapeDtypeStruct(shape, F32)


VMEM = pl.BlockSpec(memory_space=pltpu.VMEM)
SMEM = pl.BlockSpec(memory_space=pltpu.SMEM)


def on_device(
    child_field,
    child_src,
    child_type,
    child_table,
    child_parent,
    child_octant,
    theta_interp,
    phi_interp,
    shift_table,
    readers,
    parent_src,
    parent_type,
    parent_table,
):
    me = lax.axis_index("dir").astype(jnp.int32)[None]

    packed = pl.pallas_call(
        pack_kernel,
        out_shape=shaped(DIRS, SENT, LANES),
        in_specs=[VMEM] * 5,
        out_specs=VMEM,
        scratch_shapes=[pltpu.VMEM((2 * LANES, LANES), F32)],
        **params(1 << 20, 3 << 20),
    )(child_field[0], child_src[0], child_type[0], child_parent, child_octant)
    got = lax.all_to_all(packed, "dir", split_axis=0, concat_axis=0)
    got = got.reshape(DIRS * SENT, LANES)

    finer = pl.pallas_call(
        polar_kernel,
        out_shape=shaped(2 * DIRS * BOXES, LANES),
        in_specs=[VMEM] * 2,
        out_specs=VMEM,
        **params(1 << 27, 4 << 20),
    )(packed.reshape(DIRS * SENT, LANES), theta_interp)
    finer_got = lax.all_to_all(finer.reshape(DIRS, 2 * BOXES, LANES), "dir", split_axis=0, concat_axis=0)

    child_rows, parent_rows = pl.pallas_call(
        tables_kernel,
        out_shape=(shaped(LANES, 2 * LANES), shaped(TYPES * 8, LANES)),
        grid_spec=pltpu.PrefetchScalarGridSpec(
            num_scalar_prefetch=1,
            grid=(1,),
            in_specs=[
                pl.BlockSpec((TYPES, 2, LANES), lambda i, me: (0, 0, me[0] // 2)),
                pl.BlockSpec((TYPES, 2, 2 * LANES), lambda i, me: (0, 0, 0)),
            ],
            out_specs=(
                pl.BlockSpec((LANES, 2 * LANES), lambda i, me: (0, 0)),
                pl.BlockSpec((TYPES * 8, LANES), lambda i, me: (0, 0)),
            ),
        ),
        **params(1 << 20, 2 << 20),
    )(me, child_table, parent_table)

    child_rows_out = pl.pallas_call(
        child_kernel,
        out_shape=shaped(SLAB, LANES),
        in_specs=[VMEM] * 2,
        out_specs=VMEM,
        scratch_shapes=[pltpu.VMEM((ENTRIES, 8, LANES), jnp.int32)] * 2,
        **params(16 << 30, 4 << 20),
    )(got, child_rows)
    child_back = lax.all_to_all(child_rows_out.reshape(DIRS, BOXES, LANES), "dir", split_axis=0, concat_axis=0)
    child_out = pl.pallas_call(
        unpack_kernel,
        out_shape=shaped(BOXES, 2, DIRS * HALF),
        in_specs=[VMEM],
        out_specs=VMEM,
        **params(1 << 20, 2 << 20),
    )(child_back)

    parent_field, to_upper, to_lower = pl.pallas_call(
        field_kernel,
        out_shape=(shaped(PARENTS * 8, LANES), shaped(BORDER * 8, LANES), shaped(BORDER * 8, LANES)),
        grid_spec=pltpu.PrefetchScalarGridSpec(
            num_scalar_prefetch=1,
            grid=(1,),
            in_specs=[
                pl.BlockSpec((DIRS, 2 * BOXES, LANES), lambda i, me: (0, 0, 0)),
                pl.BlockSpec((DIRS * SENT, LANES), lambda i, me: (0, 0)),
                pl.BlockSpec((LANES, HALF), lambda i, me: (0, 0)),
                pl.BlockSpec((OCTANTS, 2, 2 * LANES), lambda i, me: (0, 0, me[0])),
                SMEM,
            ],
            out_specs=(
                pl.BlockSpec((PARENTS * 8, LANES), lambda i, me: (0, 0)),
                pl.BlockSpec((BORDER * 8, LANES), lambda i, me: (0, 0)),
                pl.BlockSpec((BORDER * 8, LANES), lambda i, me: (0, 0)),
            ),
            scratch_shapes=[pltpu.VMEM((PARENTS * 8, LANES), F32)],
        ),
        **params(2 << 30, 4 << 20),
    )(me, finer_got, got, phi_interp, shift_table, readers[0])
    slabs = lax.axis_size("slab")
    from_lower = lax.ppermute(to_upper, "slab", [(s, s + 1) for s in range(slabs - 1)])
    from_upper = lax.ppermute(to_lower, "slab", [(s + 1, s) for s in range(slabs - 1)])

    parent_out = pl.pallas_call(
        parent_kernel,
        out_shape=shaped(PARENTS, 2, 2 * LANES),
        in_specs=[SMEM] * 2 + [VMEM] * 4,
        out_specs=VMEM,
        scratch_shapes=[pltpu.VMEM(((PARENTS + 2 * BORDER) * 8, LANES), F32)],
        **params(1 << 28, 3 << 20),
    )(parent_src[0], parent_type[0], parent_field, from_lower, from_upper, parent_rows)
    return (child_out[None], parent_out[None])


def solution(mesh):
    return jax.shard_map(
        on_device,
        mesh=mesh,
        in_specs=(
            P("slab", "dir", None, None),
            P("slab", "dir", None),
            P("slab", "dir", None),
            P(),
            P("slab", "dir"),
            P("slab", "dir"),
            P(),
            P(),
            P(),
            P("slab", None, None),
            P("slab", None, None),
            P("slab", None, None),
            P(None, None, "dir"),
        ),
        out_specs=(P("slab", "dir", None, None), P("slab", None, None, "dir")),
        check_vma=False,
    )
```

```python
import functools

import jax
import jax.numpy as jnp
from jax import lax
from jax.experimental import pallas as pl
from jax.experimental.pallas import tpu as pltpu
from jax.sharding import PartitionSpec as P

F32 = jnp.float32
BF16 = jnp.bfloat16
I16 = jnp.int16
LANES = 128
HALF = 64
DIRS = 32
BOXES = 32
SLAB = DIRS * BOXES
ENTRIES = 24
TOGETHER = 4
GROUPS = ENTRIES // TOGETHER
AT_ONCE = 8
TYPES = 160
PARENTS = 128
BORDER = 32
OCTANTS = 8
LIST_ROWS = ENTRIES * BOXES // LANES
AT_TYPE = BOXES + LIST_ROWS
AT_OWNER = AT_TYPE + LIST_ROWS
SENT = 48

VMEM = pl.BlockSpec(memory_space=pltpu.VMEM)
SMEM = pl.BlockSpec(memory_space=pltpu.SMEM)
ANY = pl.BlockSpec(memory_space=pl.ANY)
HBM = pl.BlockSpec(memory_space=pltpu.HBM)
DMA = pltpu.SemaphoreType.DMA


def kept_out(*values):
    return tuple(pltpu.with_memory_space_constraint(value, pltpu.HBM) for value in values)


def shaped(*shape, dtype=F32):
    return jax.ShapeDtypeStruct(shape, dtype)


def call(kernel, out_shape, in_specs, out_specs, scratch, flops, nbytes, limit=24, **more):
    return pl.pallas_call(
        kernel,
        out_shape=out_shape,
        in_specs=in_specs,
        out_specs=out_specs,
        scratch_shapes=scratch,
        compiler_params=pltpu.CompilerParams(vmem_limit_bytes=limit << 20),
        cost_estimate=pl.CostEstimate(flops=flops, bytes_accessed=nbytes, transcendentals=0),
        **more,
    )


def lane_ids(rows):
    return lax.broadcasted_iota(jnp.int32, (rows, LANES), 1)


def swap_halves(value):
    return pltpu.roll(value, HALF, 1)


def split(value):
    high = value.astype(BF16)
    return high, (value - high.astype(F32)).astype(BF16)


def flat_rows(value):
    return jnp.concatenate([value[k : k + 1] for k in range(value.shape[0])], axis=1)


def one_hot(count, wanted):
    n = wanted.shape[1]
    tiled = jnp.concatenate([jnp.broadcast_to(wanted, (16, n)).astype(I16)] * (count // 16), axis=0)
    return jnp.where(lax.broadcasted_iota(I16, (count, n), 0) == tiled, BF16(1), BF16(0))


def pack_kernel(field, src, kind, parent, octant, out, held, lists, owned, packed, sems, out_sems):
    pieces = 4
    width = DIRS * HALF // pieces
    small = []
    for n, (ref, to) in enumerate(
        ((src, lists.at[0]), (kind, lists.at[1]), (parent, owned.at[0]), (octant, owned.at[1]))
    ):
        small.append(pltpu.make_async_copy(ref, to, sems.at[n]))
    large = []
    for n in range(pieces):
        cut = pl.ds(n * width, width)
        large.append(pltpu.make_async_copy(field.at[:, :, cut], held.at[:, :, cut], sems.at[4 + n]))
    for copy in small + large:
        copy.start()
    for copy in small:
        copy.wait()
    chunk = lane_ids(LIST_ROWS) // BOXES
    parts = []
    for n in range(2):
        rows = jnp.zeros((LIST_ROWS, LANES), F32)
        value = lists[n].astype(F32)
        value = jnp.concatenate([value] * 4, axis=1)
        for row in range(LIST_ROWS):
            for part in range(4):
                at = 4 * row + part
                here = (chunk == part) & (lax.broadcasted_iota(jnp.int32, (LIST_ROWS, LANES), 0) == row)
                rows = jnp.where(here, value[at : at + 1], rows)
        parts.append(rows)
    for n in range(2):
        parts.append(jnp.concatenate([owned[n].astype(F32)] * 4, axis=1))
    parts.append(jnp.zeros((SENT - AT_OWNER - 2, LANES), F32))
    tail = jnp.concatenate(parts, axis=0)
    low = lane_ids(BOXES) < HALF
    outs = []
    each = DIRS // pieces
    for n in range(pieces):
        for device in range(n * each, (n + 1) * each):
            packed[device, BOXES:SENT, :] = tail
        large[n].wait()
        for pair in range(n * each // 2, (n + 1) * each // 2):
            real = held[:, 0, pair * LANES : (pair + 1) * LANES]
            imag = held[:, 1, pair * LANES : (pair + 1) * LANES]
            packed[2 * pair, 0:BOXES, :] = jnp.where(low, real, swap_halves(imag))
            packed[2 * pair + 1, 0:BOXES, :] = jnp.where(low, swap_halves(real), imag)
        cut = pl.ds(n * each, each)
        outs.append(pltpu.make_async_copy(packed.at[cut], out.at[cut], out_sems.at[n]))
        outs[-1].start()
    for copy in outs:
        copy.wait()


def beside_kernel(
    me,
    packed,
    theta,
    child,
    kind,
    src,
    parent_table,
    out,
    child_out,
    weight_out,
    hot_out,
    held,
    table,
    sems,
):
    at = pl.multiple_of((me[0] // 2) * LANES, LANES)
    copies = [
        pltpu.make_async_copy(child.at[:, :, pl.ds(at, LANES)], held, sems.at[0]),
        pltpu.make_async_copy(parent_table, table, sems.at[1]),
    ]
    for copy in copies:
        copy.start()
    columns = [packed[pl.ds(c, DIRS, stride=SENT), :] for c in range(BOXES)]
    fields = jnp.concatenate(columns, axis=1)
    high, low = split(fields)
    theta_high, theta_low = split(theta[...])
    left = jnp.concatenate([theta_high, theta_high, theta_low], axis=1)
    right = jnp.concatenate([high, low, high], axis=0)
    finer = jnp.dot(left, right, preferred_element_type=F32)
    for c in range(BOXES):
        out[pl.ds(c, 2 * DIRS, stride=BOXES), :] = finer[:, c * LANES : (c + 1) * LANES]
    for copy in copies:
        copy.wait()
    pad = jnp.zeros((2 * LANES - TYPES, LANES), F32)
    odd = lax.rem(me[0], 2) == 1
    low = lane_ids(TYPES) < HALF
    real, imag = held[:, 0, :], held[:, 1, :]
    even_rows = jnp.where(low, real, swap_halves(imag))
    odd_rows = jnp.where(low, swap_halves(real), imag)
    rows = jnp.where(odd, odd_rows, even_rows)
    child_out[...] = jnp.transpose(jnp.concatenate([rows, pad], axis=0))
    weights = []
    for part in range(2):
        for polar in range(2):
            weight = jnp.concatenate([table[:, part, polar * LANES : (polar + 1) * LANES], pad], axis=0)
            weights.append(jnp.transpose(weight))
    weights = jnp.concatenate(split(jnp.concatenate(weights, axis=0)), axis=0)
    rows = 4 * LANES
    for n, at in enumerate(range(0, ENTRIES, TOGETHER)):
        hot_out[n] = one_hot(2 * LANES, flat_rows(src[at : at + TOGETHER, :]))
        hot = one_hot(2 * LANES, flat_rows(kind[at : at + TOGETHER, :]))
        value = jnp.dot(weights, hot, preferred_element_type=F32)
        weight_out[n] = value[:rows] + value[rows:]


def lookup(table, wanted):
    wanted = jnp.broadcast_to(wanted, (LANES, LANES))
    lanes = wanted & (LANES - 1)
    first = jnp.take_along_axis(table[:, :LANES], lanes, axis=1)
    second = jnp.take_along_axis(table[:, LANES:], lanes, axis=1)
    return jnp.where(wanted >= LANES, second, first)


def child_kernel(got, table, out, fields, src, kind):
    chunk = lane_ids(8) // BOXES
    for at, ref in ((BOXES, src), (AT_TYPE, kind)):
        for row in range(LIST_ROWS):
            rows = [got[pl.ds(i * SENT + at + row, 8, stride=4 * SENT), :] for i in range(4)]
            for part in range(4):
                value = jnp.zeros((8, LANES), F32)
                for i in range(4):
                    moved = rows[i] if i == part else pltpu.roll(rows[i], ((i - part) % 4) * BOXES, 1)
                    value = jnp.where(chunk == i, moved, value)
                ref[4 * row + part] = value.astype(jnp.int32)
    rows = jnp.concatenate([got[d * SENT : d * SENT + BOXES, :] for d in range(DIRS)], axis=0)
    fields[...] = jnp.concatenate(split(jnp.transpose(rows)), axis=0)
    tile = 2 * LANES

    def step(at, totals):
        real, imag = totals
        for n in range(AT_ONCE):
            entry = at * AT_ONCE + n
            wanted, kinds = flat_rows(src[entry]), kind[entry]
            picked = []
            for k in range(SLAB // tile):
                hot = one_hot(SLAB, wanted[:, k * tile : (k + 1) * tile])
                value = jnp.dot(fields[...], hot, preferred_element_type=F32)
                picked.append(value[:LANES] + value[LANES:])
            picked = jnp.concatenate(picked, axis=1)
            weight = jnp.concatenate([lookup(table, kinds[k : k + 1]) for k in range(8)], axis=1)
            fr, fi, wr, wi = picked[:HALF], picked[HALF:], weight[:HALF], weight[HALF:]
            real, imag = real + (wr * fr - wi * fi), imag + (wr * fi + wi * fr)
        return real, imag

    zero = jnp.zeros((HALF, SLAB), F32)
    real, imag = lax.fori_loop(0, ENTRIES // AT_ONCE, step, (zero, zero))
    out[...] = jnp.transpose(jnp.concatenate([real, imag], axis=0))


def unpack_kernel(got, out):
    low = lane_ids(BOXES) < HALF
    for pair in range(DIRS // 2):
        first, second = got[2 * pair], got[2 * pair + 1]
        out[:, 0, pair * LANES : (pair + 1) * LANES] = jnp.where(low, first, swap_halves(second))
        out[:, 1, pair * LANES : (pair + 1) * LANES] = jnp.where(low, swap_halves(first), second)


def field_kernel(me, got, owner, turn, shift_table, readers, out, up, down, shifts, sem):
    at = pl.multiple_of(me[0] * 2 * LANES, 2 * LANES)
    copy = pltpu.make_async_copy(shift_table.at[:, :, pl.ds(at, 2 * LANES)], shifts, sem)
    copy.start()
    chunk = lane_ids(8) // BOXES
    code = jnp.zeros((8, LANES), F32)
    for i in range(4):
        at = i * SENT + AT_OWNER
        parent = owner[pl.ds(at, 8, stride=4 * SENT), :]
        octant = owner[pl.ds(at + 1, 8, stride=4 * SENT), :]
        code = jnp.where(chunk == i, octant * PARENTS + parent, code)
    hot = one_hot(OCTANTS * PARENTS, flat_rows(code.astype(jnp.int32)))
    halves = []
    for polar in range(2):
        rows = [got[d, polar * BOXES : (polar + 1) * BOXES, :] for d in range(DIRS)]
        halves.extend(split(jnp.concatenate(rows, axis=0)))
    sums = jnp.dot(hot, jnp.concatenate(halves, axis=1), preferred_element_type=F32)
    none = jnp.zeros((HALF, LANES), F32)
    both = jnp.concatenate(
        [jnp.concatenate([turn[...], none], axis=1), jnp.concatenate([none, turn[...]], axis=1)], axis=0
    )
    both_high, both_low = split(both)
    right = jnp.concatenate([both_high, both_high, both_low], axis=0)
    copy.wait()
    columns = [None] * 4
    for polar in range(2):
        base = 2 * LANES * polar
        high, low = split(sums[:, base : base + LANES] + sums[:, base + LANES : base + 2 * LANES])
        fine = jnp.dot(jnp.concatenate([high, low, high], axis=1), right, preferred_element_type=F32)
        real = jnp.zeros((PARENTS, LANES), F32)
        imag = jnp.zeros((PARENTS, LANES), F32)
        for o in range(OCTANTS):
            fr = fine[o * PARENTS : (o + 1) * PARENTS, :LANES]
            fi = fine[o * PARENTS : (o + 1) * PARENTS, LANES:]
            sr = shifts[o, 0:1, polar * LANES : (polar + 1) * LANES]
            si = shifts[o, 1:2, polar * LANES : (polar + 1) * LANES]
            real += sr * fr - si * fi
            imag += sr * fi + si * fr
        columns[polar] = jnp.transpose(real)
        columns[2 + polar] = jnp.transpose(imag)
    field = jnp.concatenate(columns, axis=1)
    out[...] = field
    rows = lax.broadcasted_iota(jnp.int32, (4 * PARENTS, LANES), 0)
    lanes = lax.broadcasted_iota(jnp.int32, (4 * PARENTS, LANES), 1)
    picks = []
    for n in range(2):
        wanted = jnp.concatenate([readers[n : n + 1, :]] * 4, axis=1)
        hit = rows == (lanes // BORDER) * PARENTS + wanted
        picks.append(hit.astype(F32).astype(BF16))
    sent = jnp.dot(
        jnp.concatenate(split(field), axis=0), jnp.concatenate(picks, axis=1), preferred_element_type=F32
    )
    sent = sent[:LANES] + sent[LANES:]
    up[...] = sent[:, :LANES]
    down[...] = sent[:, LANES:]


def parent_kernel(own, lower, upper, weights, hots, out):
    lane = lane_ids(LANES)
    fields = []
    for m in range(4):
        below, above = lower[...], upper[...]
        if m > 0:
            below = pltpu.roll(below, (4 - m) * BORDER, 1)
        if m != 1:
            above = pltpu.roll(above, ((5 - m) % 4) * BORDER, 1)
        border = jnp.where(lane < BORDER, below, jnp.where(lane < 2 * BORDER, above, 0.0))
        fields.append(jnp.concatenate([own[:, m * PARENTS : (m + 1) * PARENTS], border], axis=1))
    fields = jnp.concatenate(split(jnp.concatenate(fields, axis=0)), axis=0)
    rows = 4 * LANES
    half = 2 * LANES
    real = jnp.zeros((half, PARENTS), F32)
    imag = jnp.zeros((half, PARENTS), F32)
    for group in range(GROUPS):
        picked = jnp.dot(fields, hots[group], preferred_element_type=F32)
        picked = picked[:rows] + picked[rows:]
        fr, fi, wr, wi = picked[:half], picked[half:], weights[group, :half], weights[group, half:]
        more_real = wr * fr - wi * fi
        more_imag = wr * fi + wi * fr
        for n in range(TOGETHER):
            real += more_real[:, n * PARENTS : (n + 1) * PARENTS]
            imag += more_imag[:, n * PARENTS : (n + 1) * PARENTS]
    out[:, 0, :] = jnp.transpose(real)
    out[:, 1, :] = jnp.transpose(imag)


def on_device(
    child_field,
    child_src,
    child_type,
    child_table,
    child_parent,
    child_octant,
    theta_interp,
    phi_interp,
    shift_table,
    readers,
    parent_src,
    parent_type,
    parent_table,
):
    me = lax.axis_index("dir").astype(jnp.int32)[None]

    packed = call(
        pack_kernel,
        shaped(DIRS, SENT, LANES),
        [HBM] * 5,
        HBM,
        [
            pltpu.VMEM((BOXES, 2, DIRS * HALF), F32),
            pltpu.VMEM((2, ENTRIES, BOXES), jnp.int32),
            pltpu.VMEM((2, 1, BOXES), jnp.int32),
            pltpu.VMEM((DIRS, SENT, LANES), F32),
            DMA((8,)),
            DMA((4,)),
        ],
        1 << 20,
        3 << 20,
    )(
        *kept_out(
            child_field[0],
            jnp.swapaxes(child_src[0], 0, 1),
            jnp.swapaxes(child_type[0], 0, 1),
            child_parent,
            child_octant,
        )
    )
    got = lax.all_to_all(packed, "dir", split_axis=0, concat_axis=0)
    got = got.reshape(DIRS * SENT, LANES)

    finer, child_rows, parent_weights, parent_hot = call(
        beside_kernel,
        (
            shaped(2 * DIRS * BOXES, LANES),
            shaped(LANES, 2 * LANES),
            pltpu.VMEM((GROUPS, 4 * LANES, TOGETHER * PARENTS), F32),
            pltpu.VMEM((GROUPS, 2 * LANES, TOGETHER * PARENTS), BF16),
        ),
        [SMEM, VMEM, VMEM, HBM, VMEM, VMEM, HBM],
        (VMEM,) * 4,
        [pltpu.VMEM((TYPES, 2, LANES), F32), pltpu.VMEM((TYPES, 2, 2 * LANES), F32), DMA((2,))],
        1 << 30,
        4 << 20,
        limit=32,
    )(
        me,
        packed.reshape(DIRS * SENT, LANES),
        theta_interp,
        *kept_out(child_table),
        jnp.swapaxes(parent_type[0], 0, 1),
        jnp.swapaxes(parent_src[0], 0, 1),
        *kept_out(parent_table),
    )
    finer_got = lax.all_to_all(finer.reshape(DIRS, 2 * BOXES, LANES), "dir", split_axis=0, concat_axis=0)

    child_rows_out = call(
        child_kernel,
        shaped(SLAB, LANES),
        [VMEM] * 2,
        VMEM,
        [
            pltpu.VMEM((2 * LANES, SLAB), BF16),
            pltpu.VMEM((ENTRIES, 8, LANES), jnp.int32),
            pltpu.VMEM((ENTRIES, 8, LANES), jnp.int32),
        ],
        16 << 30,
        4 << 20,
    )(got, child_rows)
    child_back = lax.all_to_all(child_rows_out.reshape(DIRS, BOXES, LANES), "dir", split_axis=0, concat_axis=0)

    own, to_upper, to_lower = call(
        field_kernel,
        (shaped(LANES, 4 * PARENTS), shaped(LANES, LANES), shaped(LANES, LANES)),
        [SMEM, VMEM, VMEM, VMEM, HBM, VMEM],
        (VMEM,) * 3,
        [pltpu.VMEM((OCTANTS, 2, 2 * LANES), F32), DMA],
        2 << 30,
        4 << 20,
    )(me, finer_got, got, jnp.swapaxes(phi_interp, 0, 1), *kept_out(shift_table), readers[0])
    slabs = lax.axis_size("slab")
    from_lower = lax.ppermute(to_upper, "slab", [(s, s + 1) for s in range(slabs - 1)])
    from_upper = lax.ppermute(to_lower, "slab", [(s + 1, s) for s in range(slabs - 1)])

    child_out = call(
        unpack_kernel, shaped(BOXES, 2, DIRS * HALF), [VMEM], VMEM, [], 1 << 20, 2 << 20
    )(child_back)

    parent_out = call(
        parent_kernel,
        shaped(PARENTS, 2, 2 * LANES),
        [VMEM] * 5,
        VMEM,
        [],
        4 << 30,
        8 << 20,
    )(own, from_lower, from_upper, parent_weights, parent_hot)
    return (child_out[None], parent_out[None])


def solution(mesh):
    return jax.shard_map(
        on_device,
        mesh=mesh,
        in_specs=(
            P("slab", "dir", None, None),
            P("slab", "dir", None),
            P("slab", "dir", None),
            P(),
            P("slab", "dir"),
            P("slab", "dir"),
            P(),
            P(),
            P(),
            P("slab", None, None),
            P("slab", None, None),
            P("slab", None, None),
            P(None, None, "dir"),
        ),
        out_specs=(P("slab", "dir", None, None), P("slab", None, None, "dir")),
        check_vma=False,
    )
```

```python
import functools

import jax
import jax.numpy as jnp
from jax import lax
from jax.experimental import pallas as pl
from jax.experimental.pallas import tpu as pltpu
from jax.sharding import PartitionSpec as P

F32 = jnp.float32
BF16 = jnp.bfloat16
I16 = jnp.int16
LANES = 128
HALF = 64
DIRS = 32
BOXES = 32
SLAB = DIRS * BOXES
ENTRIES = 24
TOGETHER = 4
GROUPS = ENTRIES // TOGETHER
AT_ONCE = 8
TYPES = 160
PARENTS = 128
BORDER = 32
OCTANTS = 8
LIST_ROWS = ENTRIES * BOXES // LANES
AT_TYPE = BOXES + LIST_ROWS
AT_OWNER = AT_TYPE + LIST_ROWS
SENT = 48

VMEM = pl.BlockSpec(memory_space=pltpu.VMEM)
SMEM = pl.BlockSpec(memory_space=pltpu.SMEM)
ANY = pl.BlockSpec(memory_space=pl.ANY)
HBM = pl.BlockSpec(memory_space=pltpu.HBM)
DMA = pltpu.SemaphoreType.DMA


def kept_out(*values):
    return tuple(pltpu.with_memory_space_constraint(value, pltpu.HBM) for value in values)


def shaped(*shape, dtype=F32):
    return jax.ShapeDtypeStruct(shape, dtype)


def call(kernel, out_shape, in_specs, out_specs, scratch, flops, nbytes, limit=24, **more):
    return pl.pallas_call(
        kernel,
        out_shape=out_shape,
        in_specs=in_specs,
        out_specs=out_specs,
        scratch_shapes=scratch,
        compiler_params=pltpu.CompilerParams(vmem_limit_bytes=limit << 20),
        cost_estimate=pl.CostEstimate(flops=flops, bytes_accessed=nbytes, transcendentals=0),
        **more,
    )


def lane_ids(rows):
    return lax.broadcasted_iota(jnp.int32, (rows, LANES), 1)


def swap_halves(value):
    return pltpu.roll(value, HALF, 1)


def split(value):
    high = value.astype(BF16)
    return high, (value - high.astype(F32)).astype(BF16)


def flat_rows(value):
    return jnp.concatenate([value[k : k + 1] for k in range(value.shape[0])], axis=1)


def one_hot(count, wanted):
    n = wanted.shape[1]
    tiled = jnp.concatenate([jnp.broadcast_to(wanted, (16, n)).astype(I16)] * (count // 16), axis=0)
    return jnp.where(lax.broadcasted_iota(I16, (count, n), 0) == tiled, BF16(1), BF16(0))


def pack_kernel(field, src, kind, parent, octant, out, held, lists, owned, packed, sems, out_sems):
    pieces = 4
    width = DIRS * HALF // pieces
    small = []
    for n, (ref, to) in enumerate(
        ((src, lists.at[0]), (kind, lists.at[1]), (parent, owned.at[0]), (octant, owned.at[1]))
    ):
        small.append(pltpu.make_async_copy(ref, to, sems.at[n]))
    large = []
    for n in range(pieces):
        cut = pl.ds(n * width, width)
        large.append(pltpu.make_async_copy(field.at[:, :, cut], held.at[:, :, cut], sems.at[4 + n]))
    for copy in small + large:
        copy.start()
    for copy in small:
        copy.wait()
    chunk = lane_ids(LIST_ROWS) // BOXES
    parts = []
    for n in range(2):
        rows = jnp.zeros((LIST_ROWS, LANES), F32)
        value = lists[n].astype(F32)
        value = jnp.concatenate([value] * 4, axis=1)
        for row in range(LIST_ROWS):
            for part in range(4):
                at = 4 * row + part
                here = (chunk == part) & (lax.broadcasted_iota(jnp.int32, (LIST_ROWS, LANES), 0) == row)
                rows = jnp.where(here, value[at : at + 1], rows)
        parts.append(rows)
    for n in range(2):
        parts.append(jnp.concatenate([owned[n].astype(F32)] * 4, axis=1))
    parts.append(jnp.zeros((SENT - AT_OWNER - 2, LANES), F32))
    tail = jnp.concatenate(parts, axis=0)
    low = lane_ids(BOXES) < HALF
    outs = []
    each = DIRS // pieces
    for n in range(pieces):
        for device in range(n * each, (n + 1) * each):
            packed[device, BOXES:SENT, :] = tail
        large[n].wait()
        for pair in range(n * each // 2, (n + 1) * each // 2):
            real = held[:, 0, pair * LANES : (pair + 1) * LANES]
            imag = held[:, 1, pair * LANES : (pair + 1) * LANES]
            packed[2 * pair, 0:BOXES, :] = jnp.where(low, real, swap_halves(imag))
            packed[2 * pair + 1, 0:BOXES, :] = jnp.where(low, swap_halves(real), imag)
        cut = pl.ds(n * each, each)
        outs.append(pltpu.make_async_copy(packed.at[cut], out.at[cut], out_sems.at[n]))
        outs[-1].start()
    for copy in outs:
        copy.wait()


def beside_kernel(
    me,
    packed,
    theta,
    child,
    kind,
    src,
    parent_table,
    out,
    child_out,
    weight_out,
    hot_out,
    held,
    table,
    sems,
):
    at = pl.multiple_of((me[0] // 2) * LANES, LANES)
    copies = [
        pltpu.make_async_copy(child.at[:, :, pl.ds(at, LANES)], held, sems.at[0]),
        pltpu.make_async_copy(parent_table, table, sems.at[1]),
    ]
    for copy in copies:
        copy.start()
    columns = [packed[pl.ds(c, DIRS, stride=SENT), :] for c in range(BOXES)]
    fields = jnp.concatenate(columns, axis=1)
    high, low = split(fields)
    theta_high, theta_low = split(theta[...])
    left = jnp.concatenate([theta_high, theta_high, theta_low], axis=1)
    right = jnp.concatenate([high, low, high], axis=0)
    finer = jnp.dot(left, right, preferred_element_type=F32)
    for c in range(BOXES):
        out[pl.ds(c, 2 * DIRS, stride=BOXES), :] = finer[:, c * LANES : (c + 1) * LANES]
    for copy in copies:
        copy.wait()
    pad = jnp.zeros((2 * LANES - TYPES, LANES), F32)
    odd = lax.rem(me[0], 2) == 1
    low = lane_ids(TYPES) < HALF
    real, imag = held[:, 0, :], held[:, 1, :]
    even_rows = jnp.where(low, real, swap_halves(imag))
    odd_rows = jnp.where(low, swap_halves(real), imag)
    rows = jnp.where(odd, odd_rows, even_rows)
    child_out[...] = jnp.transpose(jnp.concatenate([rows, pad], axis=0))
    weights = []
    for part in range(2):
        for polar in range(2):
            weight = jnp.concatenate([table[:, part, polar * LANES : (polar + 1) * LANES], pad], axis=0)
            weights.append(jnp.transpose(weight))
    weights = jnp.concatenate(split(jnp.concatenate(weights, axis=0)), axis=0)
    rows = 4 * LANES
    for n, at in enumerate(range(0, ENTRIES, TOGETHER)):
        hot_out[n] = one_hot(2 * LANES, flat_rows(src[at : at + TOGETHER, :]))
        hot = one_hot(2 * LANES, flat_rows(kind[at : at + TOGETHER, :]))
        value = jnp.dot(weights, hot, preferred_element_type=F32)
        weight_out[n] = value[:rows] + value[rows:]


def lookup(table, wanted):
    wanted = jnp.broadcast_to(wanted, (LANES, LANES))
    lanes = wanted & (LANES - 1)
    first = jnp.take_along_axis(table[:, :LANES], lanes, axis=1)
    second = jnp.take_along_axis(table[:, LANES:], lanes, axis=1)
    return jnp.where(wanted >= LANES, second, first)


def pick(exact, wanted):
    wanted = jnp.broadcast_to(wanted, (LANES, LANES))
    lanes = wanted & (LANES - 1)
    values = [
        jnp.take_along_axis(exact[:, k * LANES : (k + 1) * LANES], lanes, axis=1) for k in range(SLAB // LANES)
    ]
    bit = LANES
    while len(values) > 1:
        upper = (wanted & bit) != 0
        values = [jnp.where(upper, values[n + 1], values[n]) for n in range(0, len(values), 2)]
        bit *= 2
    return values[0]


def child_kernel(got, table, out, fields, exact, src, kind, held, sems):
    chunk = lane_ids(8) // BOXES
    for at, ref in ((BOXES, src), (AT_TYPE, kind)):
        for row in range(LIST_ROWS):
            rows = [got[pl.ds(i * SENT + at + row, 8, stride=4 * SENT), :] for i in range(4)]
            for part in range(4):
                value = jnp.zeros((8, LANES), F32)
                for i in range(4):
                    moved = rows[i] if i == part else pltpu.roll(rows[i], ((i - part) % 4) * BOXES, 1)
                    value = jnp.where(chunk == i, moved, value)
                ref[4 * row + part] = value.astype(jnp.int32)
    rows = jnp.concatenate([got[d * SENT : d * SENT + BOXES, :] for d in range(DIRS)], axis=0)
    exact[...] = jnp.transpose(rows)
    fields[...] = jnp.concatenate(split(exact[...]), axis=0)
    tile = 2 * LANES

    def step(step_at, totals):
        real, imag = totals
        for n in range(AT_ONCE):
            entry = step_at * AT_ONCE + n
            wanted, kinds = flat_rows(src[entry]), kind[entry]
            picked = []
            for k in range(SLAB // tile):
                if n % 2 == 1 and k == SLAB // tile - 1:
                    picked.extend(pick(exact, wanted[:, at : at + LANES]) for at in (k * tile, k * tile + LANES))
                    continue
                hot = one_hot(SLAB, wanted[:, k * tile : (k + 1) * tile])
                value = jnp.dot(fields[...], hot, preferred_element_type=F32)
                picked.append(value[:LANES] + value[LANES:])
            picked = jnp.concatenate(picked, axis=1)
            weight = jnp.concatenate([lookup(table, kinds[k : k + 1]) for k in range(8)], axis=1)
            fr, fi, wr, wi = picked[:HALF], picked[HALF:], weight[:HALF], weight[HALF:]
            real, imag = real + (wr * fr - wi * fi), imag + (wr * fi + wi * fr)
        return real, imag

    zero = jnp.zeros((HALF, SLAB), F32)
    real, imag = lax.fori_loop(0, ENTRIES // AT_ONCE, step, (zero, zero))
    total = jnp.concatenate([real, imag], axis=0)
    copies = []
    for n in range(4):
        cut = pl.ds(n * tile, tile)
        held[cut, :] = jnp.transpose(total[:, n * tile : (n + 1) * tile])
        copies.append(pltpu.make_async_copy(held.at[cut], out.at[cut], sems.at[n]))
        copies[-1].start()
    for copy in copies:
        copy.wait()


def unpack_kernel(got, out, held, sems):
    low = lane_ids(BOXES) < HALF
    pieces = 4
    pairs = DIRS // 2 // pieces
    copies = []
    for n in range(pieces):
        for pair in range(n * pairs, (n + 1) * pairs):
            first, second = got[2 * pair], got[2 * pair + 1]
            held[:, 0, pair * LANES : (pair + 1) * LANES] = jnp.where(low, first, swap_halves(second))
            held[:, 1, pair * LANES : (pair + 1) * LANES] = jnp.where(low, swap_halves(first), second)
        cut = pl.ds(n * pairs * LANES, pairs * LANES)
        copies.append(pltpu.make_async_copy(held.at[:, :, cut], out.at[:, :, cut], sems.at[n]))
        copies[-1].start()
    for copy in copies:
        copy.wait()


def family(owner):
    chunk = lane_ids(8) // BOXES
    code = jnp.zeros((8, LANES), F32)
    for i in range(4):
        at = i * SENT + AT_OWNER
        parent = owner[pl.ds(at, 8, stride=4 * SENT), :]
        octant = owner[pl.ds(at + 1, 8, stride=4 * SENT), :]
        code = jnp.where(chunk == i, octant * PARENTS + parent, code)
    return flat_rows(code.astype(jnp.int32))


def shifted_sums(hot, got, turn, shifts, count):
    halves = []
    for polar in range(2):
        rows = [got[d, polar * BOXES : (polar + 1) * BOXES, :] for d in range(DIRS)]
        halves.extend(split(jnp.concatenate(rows, axis=0)))
    sums = jnp.dot(hot, jnp.concatenate(halves, axis=1), preferred_element_type=F32)
    none = jnp.zeros((HALF, LANES), F32)
    both = jnp.concatenate(
        [jnp.concatenate([turn[...], none], axis=1), jnp.concatenate([none, turn[...]], axis=1)], axis=0
    )
    both_high, both_low = split(both)
    right = jnp.concatenate([both_high, both_high, both_low], axis=0)
    results = []
    for polar in range(2):
        base = 2 * LANES * polar
        high, low = split(sums[:, base : base + LANES] + sums[:, base + LANES : base + 2 * LANES])
        fine = jnp.dot(jnp.concatenate([high, low, high], axis=1), right, preferred_element_type=F32)
        real = jnp.zeros((count, LANES), F32)
        imag = jnp.zeros((count, LANES), F32)
        for o in range(OCTANTS):
            fr = fine[o * count : (o + 1) * count, :LANES]
            fi = fine[o * count : (o + 1) * count, LANES:]
            sr = shifts[o, 0:1, polar * LANES : (polar + 1) * LANES]
            si = shifts[o, 1:2, polar * LANES : (polar + 1) * LANES]
            real += sr * fr - si * fi
            imag += sr * fi + si * fr
        results.append((real, imag))
    return results


def shift_copy(me, shift_table, shifts, sem):
    at = pl.multiple_of(me[0] * 2 * LANES, 2 * LANES)
    return pltpu.make_async_copy(shift_table.at[:, :, pl.ds(at, 2 * LANES)], shifts, sem)


def border_kernel(me, got, owner, turn, shift_table, readers, up, down, shifts, sem):
    copy = shift_copy(me, shift_table, shifts, sem)
    copy.start()
    count = 2 * BORDER
    wanted = jnp.concatenate([readers[0:1, :], readers[1:2, :]], axis=1).astype(F32)
    wanted = jnp.concatenate([wanted, jnp.zeros((1, LANES - count), F32)], axis=1)
    wanted = jnp.transpose(jnp.broadcast_to(wanted, (LANES, LANES)))[:count].astype(jnp.int32)
    code = family(owner)
    blocks = []
    for k in range(SLAB // LANES):
        block = jnp.broadcast_to(code[:, k * LANES : (k + 1) * LANES], (count, LANES)).astype(I16)
        hits = []
        for o in range(OCTANTS):
            here = (wanted + o * PARENTS).astype(I16)
            hits.append(jnp.where(here == block, BF16(1), BF16(0)))
        blocks.append(jnp.concatenate(hits, axis=0))
    hot = jnp.concatenate(blocks, axis=1)
    copy.wait()
    (real0, imag0), (real1, imag1) = shifted_sums(hot, got, turn, shifts, count)
    for m, value in enumerate((real0, real1, imag0, imag1)):
        up[:, m * LANES : (m + 1) * LANES] = value[:BORDER]
        down[:, m * LANES : (m + 1) * LANES] = value[BORDER:]


def own_kernel(me, got, owner, turn, shift_table, out, shifts, sem):
    copy = shift_copy(me, shift_table, shifts, sem)
    copy.start()
    hot = one_hot(OCTANTS * PARENTS, family(owner))
    copy.wait()
    (real0, imag0), (real1, imag1) = shifted_sums(hot, got, turn, shifts, PARENTS)
    for m, value in enumerate((real0, real1, imag0, imag1)):
        out[:, m * PARENTS : (m + 1) * PARENTS] = jnp.transpose(value)


def parent_kernel(own, lower, upper, weights, hots, out):
    border = jnp.concatenate([lower[...], upper[...], jnp.zeros((2 * BORDER, 4 * LANES), F32)], axis=0)
    fields = []
    for m in range(4):
        turned = jnp.transpose(border[:, m * LANES : (m + 1) * LANES])
        fields.append(jnp.concatenate([own[:, m * PARENTS : (m + 1) * PARENTS], turned], axis=1))
    fields = jnp.concatenate(split(jnp.concatenate(fields, axis=0)), axis=0)
    rows = 4 * LANES
    half = 2 * LANES
    real = jnp.zeros((half, PARENTS), F32)
    imag = jnp.zeros((half, PARENTS), F32)
    for group in range(GROUPS):
        picked = jnp.dot(fields, hots[group], preferred_element_type=F32)
        picked = picked[:rows] + picked[rows:]
        fr, fi, wr, wi = picked[:half], picked[half:], weights[group, :half], weights[group, half:]
        more_real = wr * fr - wi * fi
        more_imag = wr * fi + wi * fr
        for n in range(TOGETHER):
            real += more_real[:, n * PARENTS : (n + 1) * PARENTS]
            imag += more_imag[:, n * PARENTS : (n + 1) * PARENTS]
    out[:, 0, :] = jnp.transpose(real)
    out[:, 1, :] = jnp.transpose(imag)


def on_device(
    child_field,
    child_src,
    child_type,
    child_table,
    child_parent,
    child_octant,
    theta_interp,
    phi_interp,
    shift_table,
    readers,
    parent_src,
    parent_type,
    parent_table,
):
    me = lax.axis_index("dir").astype(jnp.int32)[None]

    packed = call(
        pack_kernel,
        shaped(DIRS, SENT, LANES),
        [HBM] * 5,
        HBM,
        [
            pltpu.VMEM((BOXES, 2, DIRS * HALF), F32),
            pltpu.VMEM((2, ENTRIES, BOXES), jnp.int32),
            pltpu.VMEM((2, 1, BOXES), jnp.int32),
            pltpu.VMEM((DIRS, SENT, LANES), F32),
            DMA((8,)),
            DMA((4,)),
        ],
        1 << 20,
        3 << 20,
    )(
        *kept_out(
            child_field[0],
            jnp.swapaxes(child_src[0], 0, 1),
            jnp.swapaxes(child_type[0], 0, 1),
            child_parent,
            child_octant,
        )
    )
    got = lax.all_to_all(packed, "dir", split_axis=0, concat_axis=0)
    got = got.reshape(DIRS * SENT, LANES)

    finer, child_rows, parent_weights, parent_hot = call(
        beside_kernel,
        (
            shaped(2 * DIRS * BOXES, LANES),
            shaped(LANES, 2 * LANES),
            pltpu.VMEM((GROUPS, 4 * LANES, TOGETHER * PARENTS), F32),
            pltpu.VMEM((GROUPS, 2 * LANES, TOGETHER * PARENTS), BF16),
        ),
        [SMEM, VMEM, VMEM, HBM, VMEM, VMEM, HBM],
        (VMEM,) * 4,
        [pltpu.VMEM((TYPES, 2, LANES), F32), pltpu.VMEM((TYPES, 2, 2 * LANES), F32), DMA((2,))],
        1 << 30,
        4 << 20,
        limit=32,
    )(
        me,
        packed.reshape(DIRS * SENT, LANES),
        theta_interp,
        *kept_out(child_table),
        jnp.swapaxes(parent_type[0], 0, 1),
        jnp.swapaxes(parent_src[0], 0, 1),
        *kept_out(parent_table),
    )
    finer_got = lax.all_to_all(finer.reshape(DIRS, 2 * BOXES, LANES), "dir", split_axis=0, concat_axis=0)

    child_rows_out = call(
        child_kernel,
        shaped(SLAB, LANES),
        [VMEM] * 2,
        HBM,
        [
            pltpu.VMEM((2 * LANES, SLAB), BF16),
            pltpu.VMEM((LANES, SLAB), F32),
            pltpu.VMEM((ENTRIES, 8, LANES), jnp.int32),
            pltpu.VMEM((ENTRIES, 8, LANES), jnp.int32),
            pltpu.VMEM((SLAB, LANES), F32),
            DMA((4,)),
        ],
        16 << 30,
        4 << 20,
    )(got, child_rows)
    child_back = lax.all_to_all(child_rows_out.reshape(DIRS, BOXES, LANES), "dir", split_axis=0, concat_axis=0)

    turn = jnp.swapaxes(phi_interp, 0, 1)
    (shift_rows,) = kept_out(shift_table)
    to_upper, to_lower = call(
        border_kernel,
        (shaped(BORDER, 4 * LANES),) * 2,
        [SMEM, VMEM, VMEM, VMEM, HBM, VMEM],
        (VMEM,) * 2,
        [pltpu.VMEM((OCTANTS, 2, 2 * LANES), F32), DMA],
        1 << 30,
        4 << 20,
    )(me, finer_got, got, turn, shift_rows, readers[0])
    own = call(
        own_kernel,
        pltpu.VMEM((LANES, 4 * PARENTS), F32),
        [SMEM, VMEM, VMEM, VMEM, HBM],
        VMEM,
        [pltpu.VMEM((OCTANTS, 2, 2 * LANES), F32), DMA],
        2 << 30,
        4 << 20,
    )(me, finer_got, got, turn, shift_rows)
    slabs = lax.axis_size("slab")
    from_lower = lax.ppermute(to_upper, "slab", [(s, s + 1) for s in range(slabs - 1)])
    from_upper = lax.ppermute(to_lower, "slab", [(s + 1, s) for s in range(slabs - 1)])

    child_out = call(
        unpack_kernel,
        shaped(BOXES, 2, DIRS * HALF),
        [VMEM],
        HBM,
        [pltpu.VMEM((BOXES, 2, DIRS * HALF), F32), DMA((4,))],
        1 << 20,
        2 << 20,
    )(child_back)

    parent_out = call(
        parent_kernel,
        shaped(PARENTS, 2, 2 * LANES),
        [VMEM] * 5,
        VMEM,
        [],
        4 << 30,
        8 << 20,
    )(own, from_lower, from_upper, parent_weights, parent_hot)
    return (child_out[None], parent_out[None])


def solution(mesh):
    return jax.shard_map(
        on_device,
        mesh=mesh,
        in_specs=(
            P("slab", "dir", None, None),
            P("slab", "dir", None),
            P("slab", "dir", None),
            P(),
            P("slab", "dir"),
            P("slab", "dir"),
            P(),
            P(),
            P(),
            P("slab", None, None),
            P("slab", None, None),
            P("slab", None, None),
            P(None, None, "dir"),
        ),
        out_specs=(P("slab", "dir", None, None), P("slab", None, None, "dir")),
        check_vma=False,
    )
```

```python
import functools

import jax
import jax.numpy as jnp
from jax import lax
from jax.experimental import pallas as pl
from jax.experimental.pallas import tpu as pltpu
from jax.sharding import PartitionSpec as P

F32 = jnp.float32
BF16 = jnp.bfloat16
I16 = jnp.int16
LANES = 128
HALF = 64
DIRS = 32
BOXES = 32
SLAB = DIRS * BOXES
ENTRIES = 24
TOGETHER = 8
GROUPS = ENTRIES // TOGETHER
AT_ONCE = 12
TYPES = 160
PARENTS = 128
BORDER = 32
OCTANTS = 8
LIST_ROWS = ENTRIES * BOXES // LANES
AT_TYPE = BOXES + LIST_ROWS
AT_OWNER = AT_TYPE + LIST_ROWS
SENT = 48

VMEM = pl.BlockSpec(memory_space=pltpu.VMEM)
SMEM = pl.BlockSpec(memory_space=pltpu.SMEM)
ANY = pl.BlockSpec(memory_space=pl.ANY)
HBM = pl.BlockSpec(memory_space=pltpu.HBM)
DMA = pltpu.SemaphoreType.DMA


def kept_out(*values):
    return tuple(pltpu.with_memory_space_constraint(value, pltpu.HBM) for value in values)


def shaped(*shape, dtype=F32):
    return jax.ShapeDtypeStruct(shape, dtype)


def call(kernel, out_shape, in_specs, out_specs, scratch, flops, nbytes, limit=24, **more):
    return pl.pallas_call(
        kernel,
        out_shape=out_shape,
        in_specs=in_specs,
        out_specs=out_specs,
        scratch_shapes=scratch,
        compiler_params=pltpu.CompilerParams(vmem_limit_bytes=limit << 20),
        cost_estimate=pl.CostEstimate(flops=flops, bytes_accessed=nbytes, transcendentals=0),
        **more,
    )


def lane_ids(rows):
    return lax.broadcasted_iota(jnp.int32, (rows, LANES), 1)


def swap_halves(value):
    return pltpu.roll(value, HALF, 1)


def split(value):
    high = value.astype(BF16)
    return high, (value - high.astype(F32)).astype(BF16)


def flat_rows(value):
    return jnp.concatenate([value[k : k + 1] for k in range(value.shape[0])], axis=1)


def one_hot(count, wanted):
    n = wanted.shape[1]
    tiled = jnp.concatenate([jnp.broadcast_to(wanted, (16, n)).astype(I16)] * (count // 16), axis=0)
    return jnp.where(lax.broadcasted_iota(I16, (count, n), 0) == tiled, BF16(1), BF16(0))


def pack_kernel(field, src, kind, parent, octant, out, held, lists, owned, packed, sems, out_sems):
    pieces = 4
    width = DIRS * HALF // pieces
    small = []
    for n, (ref, to) in enumerate(
        ((src, lists.at[0]), (kind, lists.at[1]), (parent, owned.at[0]), (octant, owned.at[1]))
    ):
        small.append(pltpu.make_async_copy(ref, to, sems.at[n]))
    large = []
    for n in range(pieces):
        cut = pl.ds(n * width, width)
        large.append(pltpu.make_async_copy(field.at[:, :, cut], held.at[:, :, cut], sems.at[4 + n]))
    for copy in small + large:
        copy.start()
    for copy in small:
        copy.wait()
    chunk = lane_ids(LIST_ROWS) // BOXES
    parts = []
    for n in range(2):
        rows = jnp.zeros((LIST_ROWS, LANES), F32)
        value = lists[n].astype(F32)
        value = jnp.concatenate([value] * 4, axis=1)
        for row in range(LIST_ROWS):
            for part in range(4):
                at = 4 * row + part
                here = (chunk == part) & (lax.broadcasted_iota(jnp.int32, (LIST_ROWS, LANES), 0) == row)
                rows = jnp.where(here, value[at : at + 1], rows)
        parts.append(rows)
    for n in range(2):
        parts.append(jnp.concatenate([owned[n].astype(F32)] * 4, axis=1))
    parts.append(jnp.zeros((SENT - AT_OWNER - 2, LANES), F32))
    tail = jnp.concatenate(parts, axis=0)
    low = lane_ids(BOXES) < HALF
    outs = []
    each = DIRS // pieces
    for n in range(pieces):
        for device in range(n * each, (n + 1) * each):
            packed[device, BOXES:SENT, :] = tail
        large[n].wait()
        for pair in range(n * each // 2, (n + 1) * each // 2):
            real = held[:, 0, pair * LANES : (pair + 1) * LANES]
            imag = held[:, 1, pair * LANES : (pair + 1) * LANES]
            packed[2 * pair, 0:BOXES, :] = jnp.where(low, real, swap_halves(imag))
            packed[2 * pair + 1, 0:BOXES, :] = jnp.where(low, swap_halves(real), imag)
        cut = pl.ds(n * each, each)
        outs.append(pltpu.make_async_copy(packed.at[cut], out.at[cut], out_sems.at[n]))
        outs[-1].start()
    for copy in outs:
        copy.wait()


def beside_kernel(
    me,
    packed,
    theta,
    child,
    kind,
    src,
    parent_table,
    out,
    child_out,
    weight_out,
    hot_out,
    held,
    table,
    sems,
):
    at = pl.multiple_of((me[0] // 2) * LANES, LANES)
    copies = [
        pltpu.make_async_copy(child.at[:, :, pl.ds(at, LANES)], held, sems.at[0]),
        pltpu.make_async_copy(parent_table, table, sems.at[1]),
    ]
    for copy in copies:
        copy.start()
    columns = [packed[pl.ds(c, DIRS, stride=SENT), :] for c in range(BOXES)]
    fields = jnp.concatenate(columns, axis=1)
    high, low = split(fields)
    theta_high, theta_low = split(theta[...])
    left = jnp.concatenate([theta_high, theta_high, theta_low], axis=1)
    right = jnp.concatenate([high, low, high], axis=0)
    finer = jnp.dot(left, right, preferred_element_type=F32)
    for c in range(BOXES):
        out[pl.ds(c, 2 * DIRS, stride=BOXES), :] = finer[:, c * LANES : (c + 1) * LANES]
    for copy in copies:
        copy.wait()
    pad = jnp.zeros((2 * LANES - TYPES, LANES), F32)
    odd = lax.rem(me[0], 2) == 1
    low = lane_ids(TYPES) < HALF
    real, imag = held[:, 0, :], held[:, 1, :]
    even_rows = jnp.where(low, real, swap_halves(imag))
    odd_rows = jnp.where(low, swap_halves(real), imag)
    rows = jnp.where(odd, odd_rows, even_rows)
    child_out[...] = jnp.transpose(jnp.concatenate([rows, pad], axis=0))
    weights = []
    for part in range(2):
        for polar in range(2):
            weight = jnp.concatenate([table[:, part, polar * LANES : (polar + 1) * LANES], pad], axis=0)
            weights.append(jnp.transpose(weight))
    weights = jnp.concatenate(split(jnp.concatenate(weights, axis=0)), axis=0)
    rows = 4 * LANES
    for n, at in enumerate(range(0, ENTRIES, TOGETHER)):
        hot_out[n] = one_hot(2 * LANES, flat_rows(src[at : at + TOGETHER, :]))
        hot = one_hot(2 * LANES, flat_rows(kind[at : at + TOGETHER, :]))
        value = jnp.dot(weights, hot, preferred_element_type=F32)
        weight_out[n] = value[:rows] + value[rows:]


def lookup(table, wanted):
    wanted = jnp.broadcast_to(wanted, (LANES, LANES))
    lanes = wanted & (LANES - 1)
    first = jnp.take_along_axis(table[:, :LANES], lanes, axis=1)
    second = jnp.take_along_axis(table[:, LANES:], lanes, axis=1)
    return jnp.where(wanted >= LANES, second, first)


def pick(exact, wanted):
    wanted = jnp.broadcast_to(wanted, (LANES, LANES))
    lanes = wanted & (LANES - 1)
    values = [
        jnp.take_along_axis(exact[:, k * LANES : (k + 1) * LANES], lanes, axis=1) for k in range(SLAB // LANES)
    ]
    bit = LANES
    while len(values) > 1:
        upper = (wanted & bit) != 0
        values = [jnp.where(upper, values[n + 1], values[n]) for n in range(0, len(values), 2)]
        bit *= 2
    return values[0]


def child_kernel(got, table, out, fields, exact, src, kind, held, sems):
    chunk = lane_ids(8) // BOXES
    for at, ref in ((BOXES, src), (AT_TYPE, kind)):
        for row in range(LIST_ROWS):
            rows = [got[pl.ds(i * SENT + at + row, 8, stride=4 * SENT), :] for i in range(4)]
            for part in range(4):
                value = jnp.zeros((8, LANES), F32)
                for i in range(4):
                    moved = rows[i] if i == part else pltpu.roll(rows[i], ((i - part) % 4) * BOXES, 1)
                    value = jnp.where(chunk == i, moved, value)
                ref[4 * row + part] = value.astype(jnp.int32)
    rows = jnp.concatenate([got[d * SENT : d * SENT + BOXES, :] for d in range(DIRS)], axis=0)
    exact[...] = jnp.transpose(rows)
    fields[...] = jnp.concatenate(split(exact[...]), axis=0)
    tile = 2 * LANES

    def step(step_at, totals):
        real, imag = totals
        for n in range(AT_ONCE):
            entry = step_at * AT_ONCE + n
            wanted, kinds = flat_rows(src[entry]), kind[entry]
            picked = []
            for k in range(SLAB // tile):
                if n % 3 != 0 and k == SLAB // tile - 1:
                    picked.extend(pick(exact, wanted[:, at : at + LANES]) for at in (k * tile, k * tile + LANES))
                    continue
                hot = one_hot(SLAB, wanted[:, k * tile : (k + 1) * tile])
                value = jnp.dot(fields[...], hot, preferred_element_type=F32)
                picked.append(value[:LANES] + value[LANES:])
            picked = jnp.concatenate(picked, axis=1)
            weight = jnp.concatenate([lookup(table, kinds[k : k + 1]) for k in range(8)], axis=1)
            fr, fi, wr, wi = picked[:HALF], picked[HALF:], weight[:HALF], weight[HALF:]
            real, imag = real + (wr * fr - wi * fi), imag + (wr * fi + wi * fr)
        return real, imag

    zero = jnp.zeros((HALF, SLAB), F32)
    real, imag = lax.fori_loop(0, ENTRIES // AT_ONCE, step, (zero, zero))
    total = jnp.concatenate([real, imag], axis=0)
    copies = []
    for n in range(4):
        cut = pl.ds(n * tile, tile)
        held[cut, :] = jnp.transpose(total[:, n * tile : (n + 1) * tile])
        copies.append(pltpu.make_async_copy(held.at[cut], out.at[cut], sems.at[n]))
        copies[-1].start()
    for copy in copies:
        copy.wait()


def unpack_kernel(got, out, held, sems):
    low = lane_ids(BOXES) < HALF
    pieces = 4
    pairs = DIRS // 2 // pieces
    copies = []
    for n in range(pieces):
        for pair in range(n * pairs, (n + 1) * pairs):
            first, second = got[2 * pair], got[2 * pair + 1]
            held[:, 0, pair * LANES : (pair + 1) * LANES] = jnp.where(low, first, swap_halves(second))
            held[:, 1, pair * LANES : (pair + 1) * LANES] = jnp.where(low, swap_halves(first), second)
        cut = pl.ds(n * pairs * LANES, pairs * LANES)
        copies.append(pltpu.make_async_copy(held.at[:, :, cut], out.at[:, :, cut], sems.at[n]))
        copies[-1].start()
    for copy in copies:
        copy.wait()


def family(owner):
    chunk = lane_ids(8) // BOXES
    code = jnp.zeros((8, LANES), F32)
    for i in range(4):
        at = i * SENT + AT_OWNER
        parent = owner[pl.ds(at, 8, stride=4 * SENT), :]
        octant = owner[pl.ds(at + 1, 8, stride=4 * SENT), :]
        code = jnp.where(chunk == i, octant * PARENTS + parent, code)
    return flat_rows(code.astype(jnp.int32))


def shifted_sums(hot, got, turn, shifts, count):
    halves = []
    for polar in range(2):
        rows = [got[d, polar * BOXES : (polar + 1) * BOXES, :] for d in range(DIRS)]
        halves.extend(split(jnp.concatenate(rows, axis=0)))
    sums = jnp.dot(hot, jnp.concatenate(halves, axis=1), preferred_element_type=F32)
    none = jnp.zeros((HALF, LANES), F32)
    both = jnp.concatenate(
        [jnp.concatenate([turn[...], none], axis=1), jnp.concatenate([none, turn[...]], axis=1)], axis=0
    )
    both_high, both_low = split(both)
    right = jnp.concatenate([both_high, both_high, both_low], axis=0)
    results = []
    for polar in range(2):
        base = 2 * LANES * polar
        high, low = split(sums[:, base : base + LANES] + sums[:, base + LANES : base + 2 * LANES])
        fine = jnp.dot(jnp.concatenate([high, low, high], axis=1), right, preferred_element_type=F32)
        real = jnp.zeros((count, LANES), F32)
        imag = jnp.zeros((count, LANES), F32)
        for o in range(OCTANTS):
            fr = fine[o * count : (o + 1) * count, :LANES]
            fi = fine[o * count : (o + 1) * count, LANES:]
            sr = shifts[o, 0:1, polar * LANES : (polar + 1) * LANES]
            si = shifts[o, 1:2, polar * LANES : (polar + 1) * LANES]
            real += sr * fr - si * fi
            imag += sr * fi + si * fr
        results.append((real, imag))
    return results


def shift_copy(me, shift_table, shifts, sem):
    at = pl.multiple_of(me[0] * 2 * LANES, 2 * LANES)
    return pltpu.make_async_copy(shift_table.at[:, :, pl.ds(at, 2 * LANES)], shifts, sem)


def border_kernel(me, got, owner, turn, shift_table, readers, up, down, shifts, sem):
    copy = shift_copy(me, shift_table, shifts, sem)
    copy.start()
    count = 2 * BORDER
    wanted = jnp.concatenate([readers[0:1, :], readers[1:2, :]], axis=1).astype(F32)
    wanted = jnp.concatenate([wanted, jnp.zeros((1, LANES - count), F32)], axis=1)
    wanted = jnp.transpose(jnp.broadcast_to(wanted, (LANES, LANES)))[:count].astype(jnp.int32)
    code = family(owner)
    blocks = []
    for k in range(SLAB // LANES):
        block = jnp.broadcast_to(code[:, k * LANES : (k + 1) * LANES], (count, LANES)).astype(I16)
        hits = []
        for o in range(OCTANTS):
            here = (wanted + o * PARENTS).astype(I16)
            hits.append(jnp.where(here == block, BF16(1), BF16(0)))
        blocks.append(jnp.concatenate(hits, axis=0))
    hot = jnp.concatenate(blocks, axis=1)
    copy.wait()
    (real0, imag0), (real1, imag1) = shifted_sums(hot, got, turn, shifts, count)
    for m, value in enumerate((real0, real1, imag0, imag1)):
        up[:, m * LANES : (m + 1) * LANES] = value[:BORDER]
        down[:, m * LANES : (m + 1) * LANES] = value[BORDER:]


def own_kernel(me, got, owner, turn, shift_table, out, shifts, sem):
    copy = shift_copy(me, shift_table, shifts, sem)
    copy.start()
    hot = one_hot(OCTANTS * PARENTS, family(owner))
    copy.wait()
    (real0, imag0), (real1, imag1) = shifted_sums(hot, got, turn, shifts, PARENTS)
    for m, value in enumerate((real0, real1, imag0, imag1)):
        out[:, m * PARENTS : (m + 1) * PARENTS] = jnp.transpose(value)


def parent_kernel(own, lower, upper, weights, hots, out):
    border = jnp.concatenate([lower[...], upper[...], jnp.zeros((2 * BORDER, 4 * LANES), F32)], axis=0)
    fields = []
    for m in range(4):
        turned = jnp.transpose(border[:, m * LANES : (m + 1) * LANES])
        fields.append(jnp.concatenate([own[:, m * PARENTS : (m + 1) * PARENTS], turned], axis=1))
    fields = jnp.concatenate(split(jnp.concatenate(fields, axis=0)), axis=0)
    rows = 4 * LANES
    half = 2 * LANES
    real = jnp.zeros((half, PARENTS), F32)
    imag = jnp.zeros((half, PARENTS), F32)
    for group in range(GROUPS):
        picked = jnp.dot(fields, hots[group], preferred_element_type=F32)
        picked = picked[:rows] + picked[rows:]
        fr, fi, wr, wi = picked[:half], picked[half:], weights[group, :half], weights[group, half:]
        more_real = wr * fr - wi * fi
        more_imag = wr * fi + wi * fr
        for n in range(TOGETHER):
            real += more_real[:, n * PARENTS : (n + 1) * PARENTS]
            imag += more_imag[:, n * PARENTS : (n + 1) * PARENTS]
    out[:, 0, :] = jnp.transpose(real)
    out[:, 1, :] = jnp.transpose(imag)


def on_device(
    child_field,
    child_src,
    child_type,
    child_table,
    child_parent,
    child_octant,
    theta_interp,
    phi_interp,
    shift_table,
    readers,
    parent_src,
    parent_type,
    parent_table,
):
    me = lax.axis_index("dir").astype(jnp.int32)[None]

    packed = call(
        pack_kernel,
        shaped(DIRS, SENT, LANES),
        [HBM] * 5,
        HBM,
        [
            pltpu.VMEM((BOXES, 2, DIRS * HALF), F32),
            pltpu.VMEM((2, ENTRIES, BOXES), jnp.int32),
            pltpu.VMEM((2, 1, BOXES), jnp.int32),
            pltpu.VMEM((DIRS, SENT, LANES), F32),
            DMA((8,)),
            DMA((4,)),
        ],
        1 << 20,
        3 << 20,
    )(
        *kept_out(
            child_field[0],
            jnp.swapaxes(child_src[0], 0, 1),
            jnp.swapaxes(child_type[0], 0, 1),
            child_parent,
            child_octant,
        )
    )
    got = lax.all_to_all(packed, "dir", split_axis=0, concat_axis=0)
    got = got.reshape(DIRS * SENT, LANES)

    finer, child_rows, parent_weights, parent_hot = call(
        beside_kernel,
        (
            shaped(2 * DIRS * BOXES, LANES),
            shaped(LANES, 2 * LANES),
            pltpu.VMEM((GROUPS, 4 * LANES, TOGETHER * PARENTS), F32),
            pltpu.VMEM((GROUPS, 2 * LANES, TOGETHER * PARENTS), BF16),
        ),
        [SMEM, VMEM, VMEM, HBM, VMEM, VMEM, HBM],
        (VMEM,) * 4,
        [pltpu.VMEM((TYPES, 2, LANES), F32), pltpu.VMEM((TYPES, 2, 2 * LANES), F32), DMA((2,))],
        1 << 30,
        4 << 20,
        limit=32,
    )(
        me,
        packed.reshape(DIRS * SENT, LANES),
        theta_interp,
        *kept_out(child_table),
        jnp.swapaxes(parent_type[0], 0, 1),
        jnp.swapaxes(parent_src[0], 0, 1),
        *kept_out(parent_table),
    )
    finer_got = lax.all_to_all(finer.reshape(DIRS, 2 * BOXES, LANES), "dir", split_axis=0, concat_axis=0)

    child_rows_out = call(
        child_kernel,
        shaped(SLAB, LANES),
        [VMEM] * 2,
        HBM,
        [
            pltpu.VMEM((2 * LANES, SLAB), BF16),
            pltpu.VMEM((LANES, SLAB), F32),
            pltpu.VMEM((ENTRIES, 8, LANES), jnp.int32),
            pltpu.VMEM((ENTRIES, 8, LANES), jnp.int32),
            pltpu.VMEM((SLAB, LANES), F32),
            DMA((4,)),
        ],
        16 << 30,
        4 << 20,
    )(got, child_rows)
    child_back = lax.all_to_all(child_rows_out.reshape(DIRS, BOXES, LANES), "dir", split_axis=0, concat_axis=0)

    turn = jnp.swapaxes(phi_interp, 0, 1)
    (shift_rows,) = kept_out(shift_table)
    to_upper, to_lower = call(
        border_kernel,
        (shaped(BORDER, 4 * LANES),) * 2,
        [SMEM, VMEM, VMEM, VMEM, HBM, VMEM],
        (VMEM,) * 2,
        [pltpu.VMEM((OCTANTS, 2, 2 * LANES), F32), DMA],
        1 << 30,
        4 << 20,
    )(me, finer_got, got, turn, shift_rows, readers[0])
    own = call(
        own_kernel,
        pltpu.VMEM((LANES, 4 * PARENTS), F32),
        [SMEM, VMEM, VMEM, VMEM, HBM],
        VMEM,
        [pltpu.VMEM((OCTANTS, 2, 2 * LANES), F32), DMA],
        2 << 30,
        4 << 20,
    )(me, finer_got, got, turn, shift_rows)
    slabs = lax.axis_size("slab")
    from_lower = lax.ppermute(to_upper, "slab", [(s, s + 1) for s in range(slabs - 1)])
    from_upper = lax.ppermute(to_lower, "slab", [(s + 1, s) for s in range(slabs - 1)])

    child_out = call(
        unpack_kernel,
        shaped(BOXES, 2, DIRS * HALF),
        [VMEM],
        HBM,
        [pltpu.VMEM((BOXES, 2, DIRS * HALF), F32), DMA((4,))],
        1 << 20,
        2 << 20,
    )(child_back)

    parent_out = call(
        parent_kernel,
        shaped(PARENTS, 2, 2 * LANES),
        [VMEM] * 5,
        VMEM,
        [],
        4 << 30,
        8 << 20,
    )(own, from_lower, from_upper, parent_weights, parent_hot)
    return (child_out[None], parent_out[None])


def solution(mesh):
    return jax.shard_map(
        on_device,
        mesh=mesh,
        in_specs=(
            P("slab", "dir", None, None),
            P("slab", "dir", None),
            P("slab", "dir", None),
            P(),
            P("slab", "dir"),
            P("slab", "dir"),
            P(),
            P(),
            P(),
            P("slab", None, None),
            P("slab", None, None),
            P("slab", None, None),
            P(None, None, "dir"),
        ),
        out_specs=(P("slab", "dir", None, None), P("slab", None, None, "dir")),
        check_vma=False,
    )
```

```python
import functools

import jax
import jax.numpy as jnp
from jax import lax
from jax.experimental import pallas as pl
from jax.experimental.pallas import tpu as pltpu
from jax.sharding import PartitionSpec as P

F32 = jnp.float32
BF16 = jnp.bfloat16
I16 = jnp.int16
LANES = 128
HALF = 64
DIRS = 32
BOXES = 32
SLAB = DIRS * BOXES
ENTRIES = 24
TOGETHER = 8
GROUPS = ENTRIES // TOGETHER
AT_ONCE = 12
TYPES = 160
PARENTS = 128
BORDER = 32
OCTANTS = 8
LIST_ROWS = ENTRIES * BOXES // LANES
AT_TYPE = BOXES + LIST_ROWS
AT_OWNER = AT_TYPE + LIST_ROWS
SENT = 48

VMEM = pl.BlockSpec(memory_space=pltpu.VMEM)
SMEM = pl.BlockSpec(memory_space=pltpu.SMEM)
ANY = pl.BlockSpec(memory_space=pl.ANY)
HBM = pl.BlockSpec(memory_space=pltpu.HBM)
DMA = pltpu.SemaphoreType.DMA


def kept_out(*values):
    return tuple(pltpu.with_memory_space_constraint(value, pltpu.HBM) for value in values)


def shaped(*shape, dtype=F32):
    return jax.ShapeDtypeStruct(shape, dtype)


def call(kernel, out_shape, in_specs, out_specs, scratch, flops, nbytes, limit=24, **more):
    return pl.pallas_call(
        kernel,
        out_shape=out_shape,
        in_specs=in_specs,
        out_specs=out_specs,
        scratch_shapes=scratch,
        compiler_params=pltpu.CompilerParams(vmem_limit_bytes=limit << 20),
        cost_estimate=pl.CostEstimate(flops=flops, bytes_accessed=nbytes, transcendentals=0),
        **more,
    )


def lane_ids(rows):
    return lax.broadcasted_iota(jnp.int32, (rows, LANES), 1)


def swap_halves(value):
    return pltpu.roll(value, HALF, 1)


def split(value):
    high = value.astype(BF16)
    return high, (value - high.astype(F32)).astype(BF16)


def flat_rows(value):
    return jnp.concatenate([value[k : k + 1] for k in range(value.shape[0])], axis=1)


def one_hot(count, wanted):
    n = wanted.shape[1]
    tiled = jnp.concatenate([jnp.broadcast_to(wanted, (16, n)).astype(I16)] * (count // 16), axis=0)
    return jnp.where(lax.broadcasted_iota(I16, (count, n), 0) == tiled, BF16(1), BF16(0))


def pack_kernel(field, src, kind, parent, octant, out, held, lists, owned, packed, sems, out_sems):
    pieces = 4
    width = DIRS * HALF // pieces
    small = []
    for n, (ref, to) in enumerate(
        ((src, lists.at[0]), (kind, lists.at[1]), (parent, owned.at[0]), (octant, owned.at[1]))
    ):
        small.append(pltpu.make_async_copy(ref, to, sems.at[n]))
    large = []
    for n in range(pieces):
        cut = pl.ds(n * width, width)
        large.append(pltpu.make_async_copy(field.at[:, :, cut], held.at[:, :, cut], sems.at[4 + n]))
    for copy in small + large:
        copy.start()
    for copy in small:
        copy.wait()
    chunk = lane_ids(LIST_ROWS) // BOXES
    parts = []
    for n in range(2):
        rows = jnp.zeros((LIST_ROWS, LANES), F32)
        value = lists[n].astype(F32)
        value = jnp.concatenate([value] * 4, axis=1)
        for row in range(LIST_ROWS):
            for part in range(4):
                at = 4 * row + part
                here = (chunk == part) & (lax.broadcasted_iota(jnp.int32, (LIST_ROWS, LANES), 0) == row)
                rows = jnp.where(here, value[at : at + 1], rows)
        parts.append(rows)
    for n in range(2):
        parts.append(jnp.concatenate([owned[n].astype(F32)] * 4, axis=1))
    parts.append(jnp.zeros((SENT - AT_OWNER - 2, LANES), F32))
    tail = jnp.concatenate(parts, axis=0)
    low = lane_ids(BOXES) < HALF
    outs = []
    each = DIRS // pieces
    for n in range(pieces):
        for device in range(n * each, (n + 1) * each):
            packed[device, BOXES:SENT, :] = tail
        large[n].wait()
        for pair in range(n * each // 2, (n + 1) * each // 2):
            real = held[:, 0, pair * LANES : (pair + 1) * LANES]
            imag = held[:, 1, pair * LANES : (pair + 1) * LANES]
            packed[2 * pair, 0:BOXES, :] = jnp.where(low, real, swap_halves(imag))
            packed[2 * pair + 1, 0:BOXES, :] = jnp.where(low, swap_halves(real), imag)
        cut = pl.ds(n * each, each)
        outs.append(pltpu.make_async_copy(packed.at[cut], out.at[cut], out_sems.at[n]))
        outs[-1].start()
    for copy in outs:
        copy.wait()


def beside_kernel(
    me,
    packed,
    theta,
    child,
    kind,
    src,
    parent_table,
    out,
    child_out,
    weight_out,
    hot_out,
    held,
    table,
    sems,
):
    at = pl.multiple_of((me[0] // 2) * LANES, LANES)
    copies = [
        pltpu.make_async_copy(child.at[:, :, pl.ds(at, LANES)], held, sems.at[0]),
        pltpu.make_async_copy(parent_table, table, sems.at[1]),
    ]
    for copy in copies:
        copy.start()
    columns = [packed[pl.ds(c, DIRS, stride=SENT), :] for c in range(BOXES)]
    fields = jnp.concatenate(columns, axis=1)
    high, low = split(fields)
    theta_high, theta_low = split(theta[...])
    left = jnp.concatenate([theta_high, theta_high, theta_low], axis=1)
    right = jnp.concatenate([high, low, high], axis=0)
    finer = jnp.dot(left, right, preferred_element_type=F32)
    for c in range(BOXES):
        out[pl.ds(c, 2 * DIRS, stride=BOXES), :] = finer[:, c * LANES : (c + 1) * LANES]
    for copy in copies:
        copy.wait()
    pad = jnp.zeros((2 * LANES - TYPES, LANES), F32)
    odd = lax.rem(me[0], 2) == 1
    low = lane_ids(TYPES) < HALF
    real, imag = held[:, 0, :], held[:, 1, :]
    even_rows = jnp.where(low, real, swap_halves(imag))
    odd_rows = jnp.where(low, swap_halves(real), imag)
    rows = jnp.where(odd, odd_rows, even_rows)
    child_out[...] = jnp.transpose(jnp.concatenate([rows, pad], axis=0))
    weights = []
    for part in range(2):
        for polar in range(2):
            weight = jnp.concatenate([table[:, part, polar * LANES : (polar + 1) * LANES], pad], axis=0)
            weights.append(jnp.transpose(weight))
    weights = jnp.concatenate(split(jnp.concatenate(weights, axis=0)), axis=0)
    rows = 4 * LANES
    for n, at in enumerate(range(0, ENTRIES, TOGETHER)):
        hot_out[n] = one_hot(2 * LANES, flat_rows(src[at : at + TOGETHER, :]))
        hot = one_hot(2 * LANES, flat_rows(kind[at : at + TOGETHER, :]))
        value = jnp.dot(weights, hot, preferred_element_type=F32)
        weight_out[n] = value[:rows] + value[rows:]


def lookup(table, wanted):
    wanted = jnp.broadcast_to(wanted, (LANES, LANES))
    lanes = wanted & (LANES - 1)
    first = jnp.take_along_axis(table[:, :LANES], lanes, axis=1)
    second = jnp.take_along_axis(table[:, LANES:], lanes, axis=1)
    return jnp.where(wanted >= LANES, second, first)


def pick(exact, wanted):
    wanted = jnp.broadcast_to(wanted, (LANES, LANES))
    lanes = wanted & (LANES - 1)
    values = [
        jnp.take_along_axis(exact[:, k * LANES : (k + 1) * LANES], lanes, axis=1) for k in range(SLAB // LANES)
    ]
    bit = LANES
    while len(values) > 1:
        upper = (wanted & bit) != 0
        values = [jnp.where(upper, values[n + 1], values[n]) for n in range(0, len(values), 2)]
        bit *= 2
    return values[0]


def child_kernel(got, table, out, fields, exact, src, kind, held, sems):
    chunk = lane_ids(8) // BOXES
    for at, ref in ((BOXES, src), (AT_TYPE, kind)):
        for row in range(LIST_ROWS):
            rows = [got[pl.ds(i * SENT + at + row, 8, stride=4 * SENT), :] for i in range(4)]
            for part in range(4):
                value = jnp.zeros((8, LANES), F32)
                for i in range(4):
                    moved = rows[i] if i == part else pltpu.roll(rows[i], ((i - part) % 4) * BOXES, 1)
                    value = jnp.where(chunk == i, moved, value)
                ref[4 * row + part] = value.astype(jnp.int32)
    rows = jnp.concatenate([got[d * SENT : d * SENT + BOXES, :] for d in range(DIRS)], axis=0)
    exact[...] = jnp.transpose(rows)
    fields[...] = jnp.concatenate(split(exact[...]), axis=0)
    tile = 2 * LANES

    def step(step_at, totals):
        real, imag = totals
        for n in range(AT_ONCE):
            entry = step_at * AT_ONCE + n
            wanted, kinds = flat_rows(src[entry]), kind[entry]
            picked = []
            for k in range(SLAB // tile):
                if n % 3 != 0 and k == SLAB // tile - 1:
                    picked.extend(pick(exact, wanted[:, at : at + LANES]) for at in (k * tile, k * tile + LANES))
                    continue
                hot = one_hot(SLAB, wanted[:, k * tile : (k + 1) * tile])
                value = jnp.dot(fields[...], hot, preferred_element_type=F32)
                picked.append(value[:LANES] + value[LANES:])
            picked = jnp.concatenate(picked, axis=1)
            weight = jnp.concatenate([lookup(table, kinds[k : k + 1]) for k in range(8)], axis=1)
            fr, fi, wr, wi = picked[:HALF], picked[HALF:], weight[:HALF], weight[HALF:]
            real, imag = real + (wr * fr - wi * fi), imag + (wr * fi + wi * fr)
        return real, imag

    zero = jnp.zeros((HALF, SLAB), F32)
    real, imag = lax.fori_loop(0, ENTRIES // AT_ONCE, step, (zero, zero))
    total = jnp.concatenate([real, imag], axis=0)
    copies = []
    for n in range(4):
        cut = pl.ds(n * tile, tile)
        held[cut, :] = jnp.transpose(total[:, n * tile : (n + 1) * tile])
        copies.append(pltpu.make_async_copy(held.at[cut], out.at[cut], sems.at[n]))
        copies[-1].start()
    for copy in copies:
        copy.wait()


def unpack_kernel(got, out, held, sems):
    low = lane_ids(BOXES) < HALF
    pieces = 4
    pairs = DIRS // 2 // pieces
    copies = []
    for n in range(pieces):
        for pair in range(n * pairs, (n + 1) * pairs):
            first, second = got[2 * pair], got[2 * pair + 1]
            held[:, 0, pair * LANES : (pair + 1) * LANES] = jnp.where(low, first, swap_halves(second))
            held[:, 1, pair * LANES : (pair + 1) * LANES] = jnp.where(low, swap_halves(first), second)
        cut = pl.ds(n * pairs * LANES, pairs * LANES)
        copies.append(pltpu.make_async_copy(held.at[:, :, cut], out.at[:, :, cut], sems.at[n]))
        copies[-1].start()
    for copy in copies:
        copy.wait()


def family(owner):
    chunk = lane_ids(8) // BOXES
    code = jnp.zeros((8, LANES), F32)
    for i in range(4):
        at = i * SENT + AT_OWNER
        parent = owner[pl.ds(at, 8, stride=4 * SENT), :]
        octant = owner[pl.ds(at + 1, 8, stride=4 * SENT), :]
        code = jnp.where(chunk == i, octant * PARENTS + parent, code)
    return flat_rows(code.astype(jnp.int32))


def shifted_sums(hot, got, turn, shifts, count):
    halves = []
    for polar in range(2):
        rows = [got[d, polar * BOXES : (polar + 1) * BOXES, :] for d in range(DIRS)]
        halves.extend(split(jnp.concatenate(rows, axis=0)))
    sums = jnp.dot(hot, jnp.concatenate(halves, axis=1), preferred_element_type=F32)
    none = jnp.zeros((HALF, LANES), F32)
    both = jnp.concatenate(
        [jnp.concatenate([turn[...], none], axis=1), jnp.concatenate([none, turn[...]], axis=1)], axis=0
    )
    both_high, both_low = split(both)
    right = jnp.concatenate([both_high, both_high, both_low], axis=0)
    results = []
    for polar in range(2):
        base = 2 * LANES * polar
        high, low = split(sums[:, base : base + LANES] + sums[:, base + LANES : base + 2 * LANES])
        fine = jnp.dot(jnp.concatenate([high, low, high], axis=1), right, preferred_element_type=F32)
        real = jnp.zeros((count, LANES), F32)
        imag = jnp.zeros((count, LANES), F32)
        for o in range(OCTANTS):
            fr = fine[o * count : (o + 1) * count, :LANES]
            fi = fine[o * count : (o + 1) * count, LANES:]
            sr = shifts[o, 0:1, polar * LANES : (polar + 1) * LANES]
            si = shifts[o, 1:2, polar * LANES : (polar + 1) * LANES]
            real += sr * fr - si * fi
            imag += sr * fi + si * fr
        results.append((real, imag))
    return results


def shift_copy(me, shift_table, shifts, sem):
    at = pl.multiple_of(me[0] * 2 * LANES, 2 * LANES)
    return pltpu.make_async_copy(shift_table.at[:, :, pl.ds(at, 2 * LANES)], shifts, sem)


def border_kernel(me, got, owner, turn, shift_table, readers, up, down, shifts, sem):
    copy = shift_copy(me, shift_table, shifts, sem)
    copy.start()
    count = 2 * BORDER
    wanted = jnp.concatenate([readers[0:1, :], readers[1:2, :]], axis=1).astype(F32)
    wanted = jnp.concatenate([wanted, jnp.zeros((1, LANES - count), F32)], axis=1)
    wanted = jnp.transpose(jnp.broadcast_to(wanted, (LANES, LANES)))[:count].astype(jnp.int32)
    code = family(owner)
    blocks = []
    for k in range(SLAB // LANES):
        block = jnp.broadcast_to(code[:, k * LANES : (k + 1) * LANES], (count, LANES)).astype(I16)
        hits = []
        for o in range(OCTANTS):
            here = (wanted + o * PARENTS).astype(I16)
            hits.append(jnp.where(here == block, BF16(1), BF16(0)))
        blocks.append(jnp.concatenate(hits, axis=0))
    hot = jnp.concatenate(blocks, axis=1)
    copy.wait()
    (real0, imag0), (real1, imag1) = shifted_sums(hot, got, turn, shifts, count)
    for m, value in enumerate((real0, real1, imag0, imag1)):
        up[m * BORDER : (m + 1) * BORDER, :] = value[:BORDER]
        down[m * BORDER : (m + 1) * BORDER, :] = value[BORDER:]


def own_kernel(me, got, owner, turn, shift_table, out, shifts, sem):
    copy = shift_copy(me, shift_table, shifts, sem)
    copy.start()
    hot = one_hot(OCTANTS * PARENTS, family(owner))
    copy.wait()
    (real0, imag0), (real1, imag1) = shifted_sums(hot, got, turn, shifts, PARENTS)
    for m, value in enumerate((real0, real1, imag0, imag1)):
        out[:, m * PARENTS : (m + 1) * PARENTS] = jnp.transpose(value)


def parent_kernel(own, lower, upper, weights, hots, out):
    none = jnp.zeros((2 * BORDER, LANES), F32)
    fields = []
    for m in range(4):
        cut = slice(m * BORDER, (m + 1) * BORDER)
        turned = jnp.transpose(jnp.concatenate([lower[cut, :], upper[cut, :], none], axis=0))
        fields.append(jnp.concatenate([own[:, m * PARENTS : (m + 1) * PARENTS], turned], axis=1))
    fields = jnp.concatenate(split(jnp.concatenate(fields, axis=0)), axis=0)
    rows = 4 * LANES
    half = 2 * LANES
    real = jnp.zeros((half, PARENTS), F32)
    imag = jnp.zeros((half, PARENTS), F32)
    for group in range(GROUPS):
        picked = jnp.dot(fields, hots[group], preferred_element_type=F32)
        picked = picked[:rows] + picked[rows:]
        fr, fi, wr, wi = picked[:half], picked[half:], weights[group, :half], weights[group, half:]
        more_real = wr * fr - wi * fi
        more_imag = wr * fi + wi * fr
        for n in range(TOGETHER):
            real += more_real[:, n * PARENTS : (n + 1) * PARENTS]
            imag += more_imag[:, n * PARENTS : (n + 1) * PARENTS]
    out[:, 0, :] = jnp.transpose(real)
    out[:, 1, :] = jnp.transpose(imag)


def on_device(
    child_field,
    child_src,
    child_type,
    child_table,
    child_parent,
    child_octant,
    theta_interp,
    phi_interp,
    shift_table,
    readers,
    parent_src,
    parent_type,
    parent_table,
):
    me = lax.axis_index("dir").astype(jnp.int32)[None]

    packed = call(
        pack_kernel,
        shaped(DIRS, SENT, LANES),
        [HBM] * 5,
        HBM,
        [
            pltpu.VMEM((BOXES, 2, DIRS * HALF), F32),
            pltpu.VMEM((2, ENTRIES, BOXES), jnp.int32),
            pltpu.VMEM((2, 1, BOXES), jnp.int32),
            pltpu.VMEM((DIRS, SENT, LANES), F32),
            DMA((8,)),
            DMA((4,)),
        ],
        1 << 20,
        3 << 20,
    )(
        *kept_out(
            child_field[0],
            jnp.swapaxes(child_src[0], 0, 1),
            jnp.swapaxes(child_type[0], 0, 1),
            child_parent,
            child_octant,
        )
    )
    got = lax.all_to_all(packed, "dir", split_axis=0, concat_axis=0)
    got = got.reshape(DIRS * SENT, LANES)

    finer, child_rows, parent_weights, parent_hot = call(
        beside_kernel,
        (
            shaped(2 * DIRS * BOXES, LANES),
            shaped(LANES, 2 * LANES),
            pltpu.VMEM((GROUPS, 4 * LANES, TOGETHER * PARENTS), F32),
            pltpu.VMEM((GROUPS, 2 * LANES, TOGETHER * PARENTS), BF16),
        ),
        [SMEM, VMEM, VMEM, HBM, VMEM, VMEM, HBM],
        (VMEM,) * 4,
        [pltpu.VMEM((TYPES, 2, LANES), F32), pltpu.VMEM((TYPES, 2, 2 * LANES), F32), DMA((2,))],
        1 << 30,
        4 << 20,
        limit=32,
    )(
        me,
        packed.reshape(DIRS * SENT, LANES),
        theta_interp,
        *kept_out(child_table),
        jnp.swapaxes(parent_type[0], 0, 1),
        jnp.swapaxes(parent_src[0], 0, 1),
        *kept_out(parent_table),
    )
    finer_got = lax.all_to_all(finer.reshape(DIRS, 2 * BOXES, LANES), "dir", split_axis=0, concat_axis=0)

    child_rows_out = call(
        child_kernel,
        shaped(SLAB, LANES),
        [VMEM] * 2,
        HBM,
        [
            pltpu.VMEM((2 * LANES, SLAB), BF16),
            pltpu.VMEM((LANES, SLAB), F32),
            pltpu.VMEM((ENTRIES, 8, LANES), jnp.int32),
            pltpu.VMEM((ENTRIES, 8, LANES), jnp.int32),
            pltpu.VMEM((SLAB, LANES), F32),
            DMA((4,)),
        ],
        16 << 30,
        4 << 20,
    )(got, child_rows)
    child_back = lax.all_to_all(child_rows_out.reshape(DIRS, BOXES, LANES), "dir", split_axis=0, concat_axis=0)

    turn = jnp.swapaxes(phi_interp, 0, 1)
    (shift_rows,) = kept_out(shift_table)
    to_upper, to_lower = call(
        border_kernel,
        (shaped(4 * BORDER, LANES),) * 2,
        [SMEM, VMEM, VMEM, VMEM, HBM, VMEM],
        (VMEM,) * 2,
        [pltpu.VMEM((OCTANTS, 2, 2 * LANES), F32), DMA],
        1 << 30,
        4 << 20,
    )(me, finer_got, got, turn, shift_rows, readers[0])
    own = call(
        own_kernel,
        pltpu.VMEM((LANES, 4 * PARENTS), F32),
        [SMEM, VMEM, VMEM, VMEM, HBM],
        VMEM,
        [pltpu.VMEM((OCTANTS, 2, 2 * LANES), F32), DMA],
        2 << 30,
        4 << 20,
    )(me, finer_got, got, turn, shift_rows)
    slabs = lax.axis_size("slab")
    from_lower = lax.ppermute(to_upper, "slab", [(s, s + 1) for s in range(slabs - 1)])
    from_upper = lax.ppermute(to_lower, "slab", [(s + 1, s) for s in range(slabs - 1)])

    child_out = call(
        unpack_kernel,
        shaped(BOXES, 2, DIRS * HALF),
        [VMEM],
        HBM,
        [pltpu.VMEM((BOXES, 2, DIRS * HALF), F32), DMA((4,))],
        1 << 20,
        2 << 20,
    )(child_back)

    parent_out = call(
        parent_kernel,
        shaped(PARENTS, 2, 2 * LANES),
        [VMEM] * 5,
        VMEM,
        [],
        4 << 30,
        8 << 20,
    )(own, from_lower, from_upper, parent_weights, parent_hot)
    return (child_out[None], parent_out[None])


def solution(mesh):
    return jax.shard_map(
        on_device,
        mesh=mesh,
        in_specs=(
            P("slab", "dir", None, None),
            P("slab", "dir", None),
            P("slab", "dir", None),
            P(),
            P("slab", "dir"),
            P("slab", "dir"),
            P(),
            P(),
            P(),
            P("slab", None, None),
            P("slab", None, None),
            P("slab", None, None),
            P(None, None, "dir"),
        ),
        out_specs=(P("slab", "dir", None, None), P("slab", None, None, "dir")),
        check_vma=False,
    )
```
